32 devices in a mesh: dp: 16 (over z, y, core), slab: 2 (over x).
Axes of the slice: x: 2, y: 2, z: 4, core: 2. Of those that a mesh axis runs over, the one named last changes fastest.
Arguments:
- snapshots: bfloat16 [16, 64, 512, 512], P('dp', None, 'slab'), may hold values from -6 to 6
- cotangent: bfloat16 [16, 64, 512, 512], P('dp', None, 'slab'), may hold values from -6 to 6
- w_spec: float32 [32, 32, 64, 128], P('slab', 'dp'), may hold values from -0.5 to 0.5
- first_moment: float32 [32, 32, 64, 128], P('slab', 'dp'), may hold values from -6 to 6
- second_moment: float32 [32, 32, 64, 128], P('slab', 'dp'), may hold values from 0.1 to 4
- w_skip: bfloat16 [64, 64], replicated, may hold values from -0.75 to 0.75
- bias: float32 [64], replicated, may hold values from -3 to 3
Outputs:
- layer_out: bfloat16 [16, 64, 512, 512], P('dp', None, 'slab')
- new_weights: float32 [32, 32, 64, 128], P('slab', 'dp')
- new_first: float32 [32, 32, 64, 128], P('slab', 'dp')
- new_second: float32 [32, 32, 64, 128], P('slab', 'dp')
The draws below stay inside these ranges and needn't reach their ends.
All inputs are finite; a program needn't handle non-finite values.
Results may differ from the reference program's by a relative error of at most 0.001.
Values sent between devices are 32-bit elements; how exact they have to be, the bound alone decides.
A program may use at most 192 MiB of HBM per device.

```python
import math
import jax
import jax.numpy as jnp
from jax import lax

C = 64
NY = 512
NZ = 512
KY = 32
KZ = 32
B = 16


def shard_levels(stream_key, dims, shards, least, high):
    loudness = 1.0
    for dim, parts in shards:
        heights = jax.random.uniform(jax.random.fold_in(jax.random.fold_in(stream_key, 6), dim), (parts,), jnp.float32, least / len(shards), high / len(shards))
        loudness = loudness * jnp.repeat(jnp.exp(heights), dims[dim] // parts).reshape((-1,) + (1,) * (len(dims) - 1 - dim))
    return loudness


def bell_draw(key, extent, scale, reach, pieces=(), held_as=jnp.bfloat16):
    result = scale * jax.random.normal(key, extent, jnp.float32)
    if pieces:
        result = result * shard_levels(key, extent, pieces, -0.22, 0.18)
    return jnp.clip(result, -reach, reach).astype(held_as)


def setup_inputs(seed: int = 0) -> dict:
    key_of = jax.random.split(jax.random.key(seed), 8)
    return {
        "snapshots": bell_draw(key_of[0], (B, C, NY, NZ), 1.0, 6.0, ((0, 16), (2, 2))),
        "cotangent": bell_draw(key_of[1], (B, C, NY, NZ), 1.0, 6.0, ((0, 16), (2, 2))),
        "w_spec": bell_draw(key_of[2], (KZ, KY, C, 2 * C), (2 * C) ** -0.5, 0.5, ((0, 2), (1, 16)), jnp.float32),
        "first_moment": bell_draw(key_of[3], (KZ, KY, C, 2 * C), 1.0, 6.0, ((0, 2), (1, 16)), jnp.float32),
        "second_moment": jnp.clip(jnp.exp(math.log(4.0) - 3.6888794 * jax.random.uniform(key_of[4], (KZ, KY, C, 2 * C), jnp.float32) ** shard_levels(key_of[4], (KZ, KY, C, 2 * C), ((0, 2), (1, 16)), -0.2, 0.2)), 0.1, 4.0),
        "w_skip": bell_draw(key_of[5], (C, C), C ** -0.5, 0.75),
        "bias": bell_draw(key_of[6], (C,), 0.5, 3.0, (), jnp.float32),
    }


high = lax.Precision.HIGHEST
gelu_coef = 0.7978845608028654
cube_coef = 0.044715

def gelu_value(x):
    return 0.5 * x * (1.0 + jnp.tanh(gelu_coef * (x + cube_coef * x * x * x)))

def gelu_slope(x):
    tanh_val = jnp.tanh(gelu_coef * (x + cube_coef * x * x * x))
    return 0.5 * (1.0 + tanh_val) + 0.5 * x * (1.0 - tanh_val * tanh_val) * gelu_coef * (1.0 + 3.0 * cube_coef * x * x)

def mode_index():
    half = KY // 2
    return jnp.concatenate([jnp.arange(half, dtype=jnp.int32), NY - half + jnp.arange(half, dtype=jnp.int32)])

def forward_modes(field):
    along_z = jnp.fft.rfft(field, axis=2)[:, :, :KZ]
    both = jnp.fft.fft(along_z, axis=1)
    picked = jnp.take(both, mode_index(), axis=1)
    return (jnp.real(picked), jnp.imag(picked))

def inverse_modes(real_part, imag_part):
    index = mode_index()
    full_real = jnp.zeros((C, NY, NZ), jnp.float32).at[:, index, :KZ].set(real_part)
    full_imag = jnp.zeros((C, NY, NZ), jnp.float32).at[:, index, :KZ].set(imag_part)
    spectrum = lax.complex(full_real, -full_imag)
    return jnp.real(jnp.fft.fft2(spectrum, axes=(1, 2)))

def reference(snapshots, cotangent, w_spec, first_moment, second_moment, w_skip, bias):
    count = snapshots.shape[0]
    w_real = w_spec[..., :C]
    w_imag = w_spec[..., C:]
    spec_scale = 1.0 / math.sqrt(NY * NZ)
    out_scale = 1.0 / math.sqrt(KY * KZ)
    skip_weight = w_skip.astype(jnp.float32)

    def one(total, inputs):
        field_low, cot_low = inputs
        field = field_low.astype(jnp.float32)
        ur, ui = forward_modes(field)
        ur = ur * spec_scale
        ui = ui * spec_scale
        vr = jnp.einsum('ijk,kjio->ojk', ur, w_real, precision=high) - jnp.einsum('ijk,kjio->ojk', ui, w_imag, precision=high)
        vi = jnp.einsum('ijk,kjio->ojk', ur, w_imag, precision=high) + jnp.einsum('ijk,kjio->ojk', ui, w_real, precision=high)
        mixed = inverse_modes(vr, vi) * out_scale
        skip = jnp.einsum('io,iyz->oyz', skip_weight, field, precision=high)
        pre = mixed + skip + bias[:, None, None]
        out = gelu_value(pre).astype(jnp.bfloat16)
        slope = cot_low.astype(jnp.float32) * gelu_slope(pre)
        gr, gi = forward_modes(slope)
        gr = gr * out_scale
        gi = gi * out_scale
        grad_real = jnp.einsum('ijk,ojk->kjio', ur, gr, precision=high) + jnp.einsum('ijk,ojk->kjio', ui, gi, precision=high)
        grad_imag = jnp.einsum('ijk,ojk->kjio', ur, gi, precision=high) - jnp.einsum('ijk,ojk->kjio', ui, gr, precision=high)
        return (total + jnp.concatenate([grad_real, grad_imag], axis=-1), out)
    init = jnp.zeros(w_spec.shape, jnp.float32)
    total, outs = lax.scan(one, init, (snapshots, cotangent))
    grad = total / count
    new_first = 0.9 * first_moment + 0.1 * grad
    new_second = 0.95 * second_moment + 0.05 * grad * grad
    bias_first = 1.0 - 0.9 ** 10
    bias_second = 1.0 - 0.95 ** 10
    new_weights = w_spec - 0.01 * (new_first / bias_first) / (jnp.sqrt(new_second / bias_second) + 1e-08)
    return (outs, new_weights, new_first, new_second)
```

```python
import math

import jax
import jax.numpy as jnp
import ml_dtypes
import numpy as np
from jax import lax
from jax.experimental import pallas as pl
from jax.experimental.pallas import tpu as pltpu
from jax.sharding import PartitionSpec as P

NY = 512
NZ = 512
KY = 32
KZ = 32
PAIRS = KY // 2
ROWS = 16
SUB = 8

gelu_coef = 0.7978845608028654
cube_coef = 0.044715
vmem_bytes = 56 * 1024 * 1024
MESH = pl.DeviceIdType.MESH


def halves(table):
    top = table.astype(ml_dtypes.bfloat16)
    rest = (table - top.astype(np.float64)).astype(ml_dtypes.bfloat16)
    return top, rest


def z_table():
    angle = 2.0 * math.pi / NZ * (np.outer(np.arange(NZ), np.arange(KZ)) % NZ)
    return np.concatenate([np.cos(angle), -np.sin(angle)], 1)


def y_table():
    mode = np.concatenate([np.arange(0, KY, 2), np.arange(1, KY, 2)])
    freq = np.where(mode < KY // 2, mode, mode - KY)
    angle = 2.0 * math.pi / NY * (np.outer(np.arange(NY), freq) % NY)
    return np.concatenate([np.cos(angle), np.sin(angle)], 1)


def split(x):
    top = x.astype(jnp.bfloat16)
    return top, (x - top.astype(jnp.float32)).astype(jnp.bfloat16)


def mm(a, b):
    return jnp.dot(a, b, preferred_element_type=jnp.float32)


def one_hot(shape, test):
    rows = lax.broadcasted_iota(jnp.int32, shape, 0)
    columns = lax.broadcasted_iota(jnp.int32, shape, 1)
    return jnp.where(test(rows, columns), 1.0, 0.0).astype(jnp.bfloat16)


def each(count, step):
    per = 8

    @pl.loop(0, count // per)
    def _(i):
        for n in range(per):
            step(i * per + n)


def y_modes(zval, ytab):
    top, rest = split(zval)
    both = mm(ytab, jnp.concatenate([top, rest], axis=1))
    first = both[: 2 * KY]
    w = first[:, : 2 * KZ] + first[:, 2 * KZ :] + both[2 * KY :, : 2 * KZ]
    real = w[:KY, :KZ] + w[KY:, KZ:]
    imag = w[:KY, KZ:] - w[KY:, :KZ]
    return jnp.concatenate([real[:PAIRS], imag[:PAIRS], real[PAIRS:], imag[PAIRS:]], axis=1)


def halves_swapped(x):
    half = x.shape[-1] // 2
    return jnp.concatenate([x[:, half:], x[:, :half]], axis=1)


class Links:
    def __init__(self, dp, slab):
        self.dp, self.slab = dp, slab
        self.me_d, self.me_s = lax.axis_index("dp"), lax.axis_index("slab")
        self.per_j, self.per_k = KY // dp, KZ // slab
        self.owners = 2 // self.per_j

    def greet(self):
        barrier = pltpu.get_barrier_semaphore()

        @pl.loop(1, self.dp)
        def _(t):
            there = lax.rem(self.me_d + t, self.dp)
            pl.semaphore_signal(barrier, inc=1, device_id=(there, self.me_s), device_id_type=MESH)

        for t in range(1, self.slab):
            there = lax.rem(self.me_s + t, self.slab)
            pl.semaphore_signal(barrier, inc=1, device_id=(self.me_d, there), device_id_type=MESH)

    def greeted(self):
        pl.semaphore_wait(pltpu.get_barrier_semaphore(), self.dp + self.slab - 2)

    def copy(self, src, dst, send, recv, d, s):
        return pltpu.make_async_remote_copy(
            src_ref=src, dst_ref=dst, send_sem=send, recv_sem=recv,
            device_id=(d, s), device_id_type=MESH,
        )

    def pack(self, modes, part, m):
        chans = modes.shape[0] // PAIRS
        turned = modes[pl.ds(m, chans, stride=PAIRS), :].T
        for n in range(2):
            own = turned[2 * n * KZ : 2 * (n + 1) * KZ]
            rows = jnp.concatenate([own[:KZ], own[KZ:]], axis=1)
            if self.per_j == 2:
                d, place = m, n * self.per_k
            else:
                d, place = m * 2 + n, 0
            for s in range(self.slab):
                part[d, s, place : place + self.per_k, :] = rows[
                    s * self.per_k : (s + 1) * self.per_k
                ]

    def to_owner(self, modes, part, near, total, got, sems):
        near_send, near_recv, far_send, far_recv = sems
        dp, slab, me_d, me_s = self.dp, self.slab, self.me_d, self.me_s
        area = self.per_j * self.per_k

        def near_copy(d, t):
            there = lax.rem(me_s + t, slab)
            return self.copy(
                part.at[d, there], near.at[t - 1, d],
                near_send.at[t - 1, d], near_recv.at[t - 1, d], me_d, there,
            )

        def far_copy(d):
            return self.copy(
                total.at[d], got.at[pl.ds(me_d * area, area)],
                far_send.at[d], far_recv.at[me_d], d, me_s,
            )

        first = lax.div(lax.rem(me_d + 1, dp), self.owners)

        @pl.loop(0, PAIRS)
        def _(n):
            m = lax.rem(first + n, PAIRS)
            self.pack(modes, part, m)
            for q in range(self.owners):
                for t in range(1, slab):
                    near_copy(m * self.owners + q, t).start()

        def summed(d):
            value = part[d, me_s]
            for t in range(1, slab):
                near_copy(d, t).wait_recv()
                value = value + near[t - 1, d]
            return value

        @pl.loop(0, dp - 1)
        def _(n):
            d = lax.rem(me_d + 1 + n, dp)
            total[d] = summed(d)
            far_copy(d).start()

        got[pl.ds(me_d * area, area), :] = summed(me_d)

        @pl.loop(0, dp - 1)
        def _(n):
            src = lax.rem(me_d + dp - 1 - n, dp)
            self.copy(
                total.at[src], got.at[pl.ds(src * area, area)],
                far_send.at[src], far_recv.at[src], src, me_s,
            ).wait_recv()

        @pl.loop(0, dp)
        def _(d):
            for t in range(1, slab):
                near_copy(d, t).wait_send()

        @pl.loop(0, dp - 1)
        def _(n):
            far_copy(lax.rem(me_d + 1 + n, dp)).wait_send()

    def from_owner(self, values, back, spec, sems):
        near_send, near_recv, far_send, far_recv = sems
        dp, slab, me_d, me_s = self.dp, self.slab, self.me_d, self.me_s
        area = self.per_j * self.per_k

        def far_copy(d):
            return self.copy(
                values.at[pl.ds(d * area, area)], back.at[me_s, me_d],
                far_send.at[d], far_recv.at[me_d], d, me_s,
            )

        def relay(d, t):
            there = lax.rem(me_s + t, slab)
            return self.copy(
                back.at[me_s, d], back.at[me_s, d],
                near_send.at[t - 1, d], near_recv.at[t - 1, d], me_d, there,
            )

        @pl.loop(0, dp - 1)
        def _(n):
            far_copy(lax.rem(me_d + 1 + n, dp)).start()

        back[me_s, me_d] = values[pl.ds(me_d * area, area), :]
        for t in range(1, slab):
            relay(me_d, t).start()

        @pl.loop(0, dp - 1)
        def _(n):
            src = lax.rem(me_d + dp - 1 - n, dp)
            self.copy(
                values.at[pl.ds(src * area, area)], back.at[me_s, src],
                far_send.at[src], far_recv.at[src], src, me_s,
            ).wait_recv()
            for t in range(1, slab):
                relay(src, t).start()

        first = lax.div(me_d, self.owners)

        @pl.loop(0, PAIRS)
        def _(n):
            m = lax.rem(first + PAIRS - n, PAIRS)
            for q in range(self.owners):
                d = m * self.owners + q
                for t in range(1, slab):
                    source = lax.rem(me_s + slab - t, slab)
                    self.copy(
                        back.at[source, d], back.at[source, d],
                        near_send.at[t - 1, d], near_recv.at[t - 1, d], me_d, source,
                    ).wait_recv()
            self.unpack(back, spec, m)

        @pl.loop(0, dp)
        def _(d):
            for t in range(1, slab):
                relay(d, t).wait_send()

        @pl.loop(0, dp - 1)
        def _(n):
            far_copy(lax.rem(me_d + 1 + n, dp)).wait_send()

    def unpack(self, back, spec, m):
        chans = spec.shape[0] // PAIRS
        blocks = []
        for n in range(2):
            if self.per_j == 2:
                d, place = m, n * self.per_k
            else:
                d, place = m * 2 + n, 0
            rows = jnp.concatenate(
                [back[s, d, place : place + self.per_k, :] for s in range(self.slab)], axis=0
            )
            blocks += [rows[:, :chans], rows[:, chans:]]
        spec[pl.ds(m, chans, stride=PAIRS), :] = jnp.concatenate(blocks, axis=0).T


def forward_kernel(
    dp, slab, x_ref, zt_ref, yt_ref, w_ref, spec_ref, u_ref,
    modes, part, near, total, got, mixer, values, back, *sems,
):
    links = Links(dp, slab)
    step = pl.program_id(0)
    per, rows, length = x_ref.shape
    chans = modes.shape[0] // PAIRS
    area = links.per_j * links.per_k

    @pl.when(step == 0)
    def _():
        links.greet()

    zval = mm(x_ref[...].reshape(per * rows, length), zt_ref[...])
    zval = (zval[:, : 2 * KZ] + zval[:, 2 * KZ :]).reshape(per, rows, 2 * KZ)
    ytab = yt_ref[links.me_s]
    for c in range(per):
        place = pl.multiple_of((step * per + c) * PAIRS, PAIRS)
        modes[pl.ds(place, PAIRS), :] = y_modes(zval[c], ytab)

    @pl.when(step == pl.num_programs(0) - 1)
    def _():
        @pl.loop(0, area)
        def _(r):
            w = w_ref[lax.rem(r, links.per_k), lax.div(r, links.per_k)]
            low = lax.broadcasted_iota(jnp.int32, w.shape, 1) < chans
            turned = halves_swapped(w)
            both = jnp.concatenate([w, jnp.where(low, -turned, turned)], axis=0)
            top, rest = split(both)
            mixer[r] = jnp.concatenate([top, rest], axis=1)

        links.greeted()
        links.to_owner(modes, part, near, total, got, sems[:4])
        scale = 1.0 / math.sqrt(NY * NZ) / math.sqrt(KY * KZ)

        @pl.loop(0, area)
        def _(r):
            u = got[pl.ds(r, dp, stride=area), :]
            top, rest = split(u)
            out = mm(jnp.concatenate([top, rest], axis=0), mixer[r])
            wide = 2 * chans
            v = out[:dp, :wide] + out[:dp, wide:] + out[dp:, :wide]
            values[pl.ds(r, dp, stride=area), :] = v * scale

        u_ref[...] = got[...]
        links.from_owner(values, back, spec_ref, sems[4:])


def grad_kernel(
    dp, slab, g_ref, u_ref, grad_ref, part, near, total, got, left, *sems
):
    links = Links(dp, slab)
    chans = g_ref.shape[0] // PAIRS
    area = links.per_j * links.per_k
    links.greet()

    @pl.loop(0, area)
    def _(r):
        turned = u_ref[pl.ds(r, dp, stride=area), :].T
        top, rest = split(jnp.concatenate([turned[:chans], turned[chans:]], axis=1))
        left[r] = jnp.concatenate([top, top, rest], axis=1)

    links.greeted()
    links.to_owner(g_ref, part, near, total, got, sems)
    scale = 1.0 / math.sqrt(NY * NZ) / math.sqrt(KY * KZ) / dp

    @pl.loop(0, area)
    def _(r):
        g = got[pl.ds(r, dp, stride=area), :]
        low = lax.broadcasted_iota(jnp.int32, g.shape, 1) < chans
        turned = halves_swapped(g)
        top, rest = split(jnp.concatenate([g, jnp.where(low, turned, -turned)], axis=0))
        grad = mm(left[r], jnp.concatenate([top, rest, top], axis=0))
        grad_ref[lax.rem(r, links.per_k), lax.div(r, links.per_k)] = grad * scale


def point_kernel(
    x_ref, cot_ref, spec_ref, bias_ref, skip_ref, zt_ref, yt_ref, back_ref, yback_ref,
    out_ref, g_ref, left, zsum, kron_ref,
):
    step = pl.program_id(0)
    chans, rows = left.shape[:2]
    wide = 2 * KZ
    me_s = lax.axis_index("slab")

    @pl.when(step == 0)
    def _():
        tall = chans * SUB
        part = tall // 4
        spread = one_hot((chans, tall), lambda i, r: i == r // SUB)
        for m in range(4):
            pick = one_hot((part, chans), lambda r, o: (r + m * part) // SUB == o)
            rows_of = mm(pick, skip_ref[...]).astype(jnp.bfloat16)
            same = one_hot((part, tall), lambda r, s: r % SUB == s % SUB)
            kron_ref[m * part : (m + 1) * part, :] = (
                mm(rows_of, spread).astype(jnp.bfloat16) * same
            )
        yback = yback_ref[me_s]

        def invert(o):
            pairs = spec_ref[pl.ds(pl.multiple_of(o * PAIRS, PAIRS), PAIRS), :]
            v = jnp.concatenate([pairs[:, :wide], pairs[:, wide:]], axis=0)
            turned = jnp.concatenate([-v[:, KZ:], v[:, :KZ]], axis=1)
            top, rest = split(jnp.concatenate([v, turned], axis=0))
            yval = mm(yback, jnp.concatenate([top, rest, top], axis=0))
            ytop, yrest = split(yval)
            b = bias_ref[o]
            b0 = b.astype(jnp.bfloat16).astype(jnp.float32)
            b1 = (b - b0).astype(jnp.bfloat16).astype(jnp.float32)
            lane = lax.broadcasted_iota(jnp.int32, b.shape, 1)
            terms = jnp.where(lane == 0, b0, jnp.where(lane == 1, b1, b - b0 - b1))
            terms = jnp.broadcast_to(terms, (rows, wide)).astype(jnp.bfloat16)
            left[o] = jnp.concatenate([ytop, yrest, ytop, terms], axis=1)

        each(chans, invert)

    here = pl.ds(pl.multiple_of(step * ROWS, ROWS), ROWS)
    field = x_ref[...].astype(jnp.float32)
    terms = left[:, here, :].astype(jnp.float32)
    values = []
    for m in range(ROWS // SUB):
        own = slice(m * SUB, (m + 1) * SUB)
        x = field[:, own].reshape(chans * SUB, NZ).astype(jnp.bfloat16)
        term = terms[:, own].reshape(chans * SUB, 4 * wide).astype(jnp.bfloat16)
        pre = mm(kron_ref[...], x) + mm(term, back_ref[...])
        sq = pre * pre
        t = jnp.tanh(pre * (gelu_coef + (gelu_coef * cube_coef) * sq))
        h = 0.5 + 0.5 * t
        value = pre * h
        values.append(value.reshape(chans, SUB, NZ))
        grow = 2.0 * gelu_coef + (6.0 * gelu_coef * cube_coef) * sq
        cot = cot_ref[...].astype(jnp.float32)[:, own].reshape(chans * SUB, NZ)
        slope = cot * (h + value * (0.5 - 0.5 * t) * grow)
        top, rest = split(slope)
        zval = mm(top, zt_ref[...])
        zval = zval[:, :wide] + zval[:, wide:] + mm(rest, zt_ref[:, :wide])
        place = pl.ds(pl.multiple_of(step * ROWS + m * SUB, SUB), SUB)
        zsum[:, place, :] = zval.reshape(chans, SUB, wide)
    out_ref[...] = jnp.concatenate(values, axis=1).astype(jnp.bfloat16)

    @pl.when(step == pl.num_programs(0) - 1)
    def _():
        ytab = yt_ref[me_s]

        def forward(o):
            place = pl.multiple_of(o * PAIRS, PAIRS)
            g_ref[pl.ds(place, PAIRS), :] = y_modes(zsum[o], ytab)

        each(chans, forward)


def whole(shape):
    return pl.BlockSpec(shape, lambda i: (0,) * len(shape))


def link_scratch(dp, slab, chans):
    area = (KY // dp) * (KZ // slab)
    wide = 2 * chans
    return [
        pltpu.VMEM((dp, slab, area, wide), jnp.float32),
        pltpu.VMEM((slab - 1, dp, area, wide), jnp.float32),
        pltpu.VMEM((dp, area, wide), jnp.float32),
        pltpu.VMEM((dp * area, wide), jnp.float32),
    ]


def link_sems(dp, slab):
    return [
        pltpu.SemaphoreType.DMA((slab - 1, dp)),
        pltpu.SemaphoreType.DMA((slab - 1, dp)),
        pltpu.SemaphoreType.DMA((dp,)),
        pltpu.SemaphoreType.DMA((dp,)),
    ]


def forward_part(field, zt, yt, w_spec, dp, slab):
    chans, rows, length = field.shape
    per = 8
    area = (KY // dp) * (KZ // slab)
    wide = 2 * chans

    def kernel(*refs):
        forward_kernel(dp, slab, *refs)

    return pl.pallas_call(
        kernel,
        grid=(chans // per,),
        in_specs=[
            pl.BlockSpec((per, rows, length), lambda i: (i, 0, 0)),
            whole(zt.shape),
            whole(yt.shape),
            whole(w_spec.shape),
        ],
        out_specs=[whole((chans * PAIRS, 4 * KZ)), whole((dp * area, wide))],
        out_shape=[
            jax.ShapeDtypeStruct((chans * PAIRS, 4 * KZ), jnp.float32),
            jax.ShapeDtypeStruct((dp * area, wide), jnp.float32),
        ],
        scratch_shapes=[pltpu.VMEM((chans * PAIRS, 4 * KZ), jnp.float32)]
        + link_scratch(dp, slab, chans)
        + [
            pltpu.VMEM((area, wide, 2 * wide), jnp.bfloat16),
            pltpu.VMEM((dp * area, wide), jnp.float32),
            pltpu.VMEM((slab, dp, area, wide), jnp.float32),
        ]
        + link_sems(dp, slab)
        + link_sems(dp, slab),
        compiler_params=pltpu.CompilerParams(
            vmem_limit_bytes=vmem_bytes, collective_id=0, has_side_effects=True
        ),
    )(field, zt, yt, w_spec)


def grad_part(gmodes, u, dp, slab):
    chans = gmodes.shape[0] // PAIRS
    per_j, per_k = KY // dp, KZ // slab
    inside = pl.BlockSpec(memory_space=pltpu.VMEM)

    def kernel(*refs):
        grad_kernel(dp, slab, *refs)

    return pl.pallas_call(
        kernel,
        in_specs=[inside, inside],
        out_specs=inside,
        out_shape=jax.ShapeDtypeStruct((per_k, per_j, chans, 2 * chans), jnp.float32),
        scratch_shapes=link_scratch(dp, slab, chans)
        + [pltpu.VMEM((per_j * per_k, chans, 6 * dp), jnp.bfloat16)]
        + link_sems(dp, slab),
        compiler_params=pltpu.CompilerParams(
            vmem_limit_bytes=vmem_bytes, collective_id=1, has_side_effects=True
        ),
    )(gmodes, u)


def point_part(field, cot, spec, bias, skip, zt, yt, back, yback):
    chans, rows, length = field.shape
    rowed = pl.BlockSpec((chans, ROWS, length), lambda i: (0, i, 0))
    return pl.pallas_call(
        point_kernel,
        grid=(rows // ROWS,),
        in_specs=[rowed, rowed]
        + [whole(a.shape) for a in (spec, bias, skip, zt, yt, back, yback)],
        out_specs=[rowed, whole((chans * PAIRS, 4 * KZ))],
        out_shape=[
            jax.ShapeDtypeStruct(field.shape, jnp.bfloat16),
            jax.ShapeDtypeStruct((chans * PAIRS, 4 * KZ), jnp.float32),
        ],
        scratch_shapes=[
            pltpu.VMEM((chans, rows, 8 * KZ), jnp.bfloat16),
            pltpu.VMEM((chans, rows, 2 * KZ), jnp.float32),
            pltpu.VMEM((chans * SUB, chans * SUB), jnp.bfloat16),
        ],
        compiler_params=pltpu.CompilerParams(vmem_limit_bytes=vmem_bytes),
    )(field, cot, spec, bias, skip, zt, yt, back, yback)


def body(snapshots, cotangent, w_spec, first_moment, second_moment, w_skip, bias):
    chans, rows, length = snapshots.shape[1:]
    dp = lax.axis_size("dp")
    slab = lax.axis_size("slab")
    ztop, zrest = halves(z_table())
    ytop, yrest = halves(y_table())
    zt = jnp.asarray(np.concatenate([ztop, zrest], 1))
    ones = np.zeros((2 * KZ, length), ml_dtypes.bfloat16)
    ones[:3] = 1
    back = jnp.asarray(np.concatenate([ztop.T, ztop.T, zrest.T, ones], 0))
    yt = np.concatenate([ytop, yrest], 1).reshape(slab, rows, -1)
    yt = jnp.asarray(np.ascontiguousarray(yt.transpose(0, 2, 1)))
    yback = jnp.asarray(np.concatenate([ytop, ytop, yrest], 1).reshape(slab, rows, -1))
    bias_lanes = jnp.pad(
        jnp.broadcast_to(bias[:, None, None], (chans, 1, 3)), ((0, 0), (0, 0), (0, 2 * KZ - 3))
    )

    spec, u = forward_part(snapshots[0], zt, yt, w_spec, dp, slab)
    layer_out, gmodes = point_part(
        snapshots[0], cotangent[0], spec, bias_lanes, w_skip.T, zt, yt, back, yback
    )
    grad = grad_part(gmodes, u, dp, slab)
    new_first = 0.9 * first_moment + 0.1 * grad
    new_second = 0.95 * second_moment + 0.05 * grad * grad
    bias_first = 1.0 - 0.9**10
    bias_second = 1.0 - 0.95**10
    new_weights = w_spec - 0.01 * (new_first / bias_first) / (
        jnp.sqrt(new_second / bias_second) + 1e-08
    )
    return (layer_out[None], new_weights, new_first, new_second)


def solution(mesh):
    placed = (
        P("dp", None, "slab", None),
        P("dp", None, "slab", None),
        P("slab", "dp", None, None),
        P("slab", "dp", None, None),
        P("slab", "dp", None, None),
        P(),
        P(),
    )
    return jax.shard_map(
        body,
        mesh=mesh,
        in_specs=placed,
        out_specs=(
            P("dp", None, "slab", None),
            P("slab", "dp", None, None),
            P("slab", "dp", None, None),
            P("slab", "dp", None, None),
        ),
        check_vma=False,
    )
```

```python
import math

import jax
import jax.numpy as jnp
import ml_dtypes
import numpy as np
from jax import lax
from jax.experimental import pallas as pl
from jax.experimental.pallas import tpu as pltpu
from jax.sharding import PartitionSpec as P

NY = 512
NZ = 512
KY = 32
KZ = 32
PAIRS = KY // 2
ROWS = 16
SUB = 8

gelu_coef = 0.7978845608028654
cube_coef = 0.044715
vmem_bytes = 56 * 1024 * 1024
MESH = pl.DeviceIdType.MESH


def halves(table):
    top = table.astype(ml_dtypes.bfloat16)
    rest = (table - top.astype(np.float64)).astype(ml_dtypes.bfloat16)
    return top, rest


def z_table():
    angle = 2.0 * math.pi / NZ * (np.outer(np.arange(NZ), np.arange(KZ)) % NZ)
    return np.concatenate([np.cos(angle), -np.sin(angle)], 1)


def y_table(mode):
    freq = np.where(mode < KY // 2, mode, mode - KY)
    angle = 2.0 * math.pi / NY * (np.outer(np.arange(NY), freq) % NY)
    return np.concatenate([np.cos(angle), np.sin(angle)], 1)


def split(x):
    top = x.astype(jnp.bfloat16)
    return top, (x - top.astype(jnp.float32)).astype(jnp.bfloat16)


def mm(a, b):
    return jnp.dot(a, b, preferred_element_type=jnp.float32)


def one_hot(shape, test):
    rows = lax.broadcasted_iota(jnp.int32, shape, 0)
    columns = lax.broadcasted_iota(jnp.int32, shape, 1)
    return jnp.where(test(rows, columns), 1.0, 0.0).astype(jnp.bfloat16)


def each(count, step):
    per = math.gcd(count, 8)

    @pl.loop(0, count // per)
    def _(i):
        for n in range(per):
            step(i * per + n)


def halves_swapped(x):
    half = x.shape[-1] // 2
    return jnp.concatenate([x[:, half:], x[:, :half]], axis=1)


def y_modes(both, ytab, slab):
    both = mm(ytab, both)
    first = both[: 2 * KY]
    w = first[:, : 2 * KZ] + first[:, 2 * KZ :] + both[2 * KY :, : 2 * KZ]
    per_k = KZ // slab
    group = 64 // per_k
    count = KY // group
    lane = lax.broadcasted_iota(jnp.int32, (KY, 2 * KZ), 1)
    real = lane % (2 * per_k) < per_k
    sine = w[KY:]
    ahead = jnp.concatenate([sine[:, per_k:], sine[:, :per_k]], axis=1)
    behind = jnp.concatenate([sine[:, 2 * KZ - per_k :], sine[:, : 2 * KZ - per_k]], axis=1)
    out = w[:KY] + jnp.where(real, ahead, -behind)
    return [
        jnp.concatenate(
            [
                out[g * count : (g + 1) * count, s * 2 * per_k : (s + 1) * 2 * per_k]
                for g in range(group)
            ],
            axis=1,
        )
        for s in range(slab)
    ]


class Links:
    def __init__(self, dp, slab):
        self.dp, self.slab = dp, slab
        self.me_d, self.me_s = lax.axis_index("dp"), lax.axis_index("slab")
        self.per_j, self.per_k = KY // dp, KZ // slab
        self.area = self.per_j * self.per_k
        self.group = 64 // self.per_k
        self.count = KY // self.group

    def greet(self):
        barrier = pltpu.get_barrier_semaphore()

        @pl.loop(1, self.dp)
        def _(t):
            there = lax.rem(self.me_d + t, self.dp)
            pl.semaphore_signal(barrier, inc=1, device_id=(there, self.me_s), device_id_type=MESH)

        for t in range(1, self.slab):
            there = lax.rem(self.me_s + t, self.slab)
            pl.semaphore_signal(barrier, inc=1, device_id=(self.me_d, there), device_id_type=MESH)

    def greeted(self):
        pl.semaphore_wait(pltpu.get_barrier_semaphore(), self.dp + self.slab - 2)

    def copy(self, src, dst, send, recv, d, s):
        return pltpu.make_async_remote_copy(
            src_ref=src, dst_ref=dst, send_sem=send, recv_sem=recv,
            device_id=(d, s), device_id_type=MESH,
        )

    def near_copy(self, step, rows, part, near, sems, t):
        there = lax.rem(self.me_s + t, self.slab)
        own = pl.ds(pl.multiple_of(step * rows, rows), rows)
        return self.copy(
            part.at[there, own], near.at[t - 1, own],
            sems[0].at[t - 1, step], sems[1].at[t - 1, step], self.me_d, there,
        )

    def chunk(self, step, per, halves_of, ytab, part, near, sems):
        rows = per * self.count
        start = pl.multiple_of(step * rows, rows)
        for c in range(per):
            for s, value in enumerate(y_modes(halves_of(c), ytab, self.slab)):
                part[s, pl.ds(start + c * self.count, self.count), :] = value

        @pl.when(step == 0)
        def _():
            self.greeted()

        for t in range(1, self.slab):
            self.near_copy(step, rows, part, near, sems, t).start()

    def to_owner(self, steps, part, near, total, got, sems):
        far_send, far_recv = sems[2:]
        dp, slab, me_d, me_s, area = self.dp, self.slab, self.me_d, self.me_s, self.area
        rows = part.shape[1] // steps
        chans = part.shape[1] // self.count

        @pl.loop(0, steps)
        def _(step):
            for t in range(1, slab):
                self.near_copy(step, rows, part, near, sems, t).wait_recv()

        def far_copy(d):
            return self.copy(
                total.at[d], got.at[pl.ds(me_d * area, area)],
                far_send.at[d], far_recv.at[me_d], d, me_s,
            )

        owners = self.group // self.per_j
        first = lax.div(lax.rem(me_d + 1, dp), owners)

        @pl.loop(0, self.count)
        def _(n):
            q = lax.rem(first + n, self.count)
            own = pl.ds(q, chans, stride=self.count)
            value = part[me_s, own, :]
            for t in range(1, slab):
                value = value + near[t - 1, own, :]
            turned = value.T
            for g in range(self.group):
                block = turned[2 * g * self.per_k : 2 * (g + 1) * self.per_k]
                place = (g % self.per_j) * self.per_k
                d = q * owners + g // self.per_j
                total[d, place : place + self.per_k, :] = jnp.concatenate(
                    [block[: self.per_k], block[self.per_k :]], axis=1
                )
            for g in range(owners):
                d = q * owners + g

                @pl.when(d != me_d)
                def _():
                    far_copy(d).start()

        got[pl.ds(me_d * area, area), :] = total[me_d]

        @pl.loop(0, dp - 1)
        def _(n):
            src = lax.rem(me_d + dp - 1 - n, dp)
            self.copy(
                total.at[src], got.at[pl.ds(src * area, area)],
                far_send.at[src], far_recv.at[src], src, me_s,
            ).wait_recv()

        @pl.loop(0, steps)
        def _(step):
            for t in range(1, slab):
                self.near_copy(step, rows, part, near, sems, t).wait_send()

        @pl.loop(0, dp - 1)
        def _(n):
            far_copy(lax.rem(me_d + 1 + n, dp)).wait_send()

    def from_owner(self, values, back, spec, sems):
        near_send, near_recv, far_send, far_recv = sems
        dp, slab, me_d, me_s, area = self.dp, self.slab, self.me_d, self.me_s, self.area

        def far_copy(d):
            return self.copy(
                values.at[pl.ds(d * area, area)], back.at[me_s, me_d],
                far_send.at[d], far_recv.at[me_d], d, me_s,
            )

        def relay(d, t):
            there = lax.rem(me_s + t, slab)
            return self.copy(
                back.at[me_s, d], back.at[me_s, d],
                near_send.at[t - 1, d], near_recv.at[t - 1, d], me_d, there,
            )

        @pl.loop(0, dp - 1)
        def _(n):
            far_copy(lax.rem(me_d + 1 + n, dp)).start()

        back[me_s, me_d] = values[pl.ds(me_d * area, area), :]
        for t in range(1, slab):
            relay(me_d, t).start()

        @pl.loop(0, dp - 1)
        def _(n):
            src = lax.rem(me_d + dp - 1 - n, dp)
            self.copy(
                values.at[pl.ds(src * area, area)], back.at[me_s, src],
                far_send.at[src], far_recv.at[src], src, me_s,
            ).wait_recv()
            for t in range(1, slab):
                relay(src, t).start()

        owners = 2 // self.per_j
        first = lax.div(me_d, owners)

        @pl.loop(0, PAIRS)
        def _(n):
            m = lax.rem(first + PAIRS - n, PAIRS)
            for q in range(owners):
                d = m * owners + q
                for t in range(1, slab):
                    source = lax.rem(me_s + slab - t, slab)
                    self.copy(
                        back.at[source, d], back.at[source, d],
                        near_send.at[t - 1, d], near_recv.at[t - 1, d], me_d, source,
                    ).wait_recv()
            self.unpack(back, spec, m)

        @pl.loop(0, dp)
        def _(d):
            for t in range(1, slab):
                relay(d, t).wait_send()

        @pl.loop(0, dp - 1)
        def _(n):
            far_copy(lax.rem(me_d + 1 + n, dp)).wait_send()

    def unpack(self, back, spec, m):
        chans = spec.shape[0] // PAIRS
        blocks = []
        for n in range(2):
            if self.per_j == 2:
                d, place = m, n * self.per_k
            else:
                d, place = m * 2 + n, 0
            rows = jnp.concatenate(
                [back[s, d, place : place + self.per_k, :] for s in range(self.slab)], axis=0
            )
            blocks += [rows[:, :chans], rows[:, chans:]]
        spec[pl.ds(m, chans, stride=PAIRS), :] = jnp.concatenate(blocks, axis=0).T


def forward_kernel(
    dp, slab, x_ref, zt_ref, yt_ref, w_ref, spec_ref, u_ref,
    part, near, total, got, mixer, values, back, *sems,
):
    links = Links(dp, slab)
    step = pl.program_id(0)
    per, rows, length = x_ref.shape
    chans = part.shape[1] // links.count
    area = links.area
    steps = chans // per

    @pl.when(step == 0)
    def _():
        links.greet()

    zval = mm(x_ref[...].reshape(per * rows, length), zt_ref[...])
    zval = (zval[:, : 2 * KZ] + zval[:, 2 * KZ :]).reshape(per, rows, 2 * KZ)

    def halves_of(c):
        return jnp.concatenate(split(zval[c]), axis=1)

    links.chunk(step, per, halves_of, yt_ref[links.me_s], part, near, sems[:4])

    @pl.when(step == pl.num_programs(0) - 1)
    def _():
        def prepare(r):
            w = w_ref[lax.rem(r, links.per_k), lax.div(r, links.per_k)]
            low = lax.broadcasted_iota(jnp.int32, w.shape, 1) < chans
            turned = halves_swapped(w)
            both = jnp.concatenate([w, jnp.where(low, -turned, turned)], axis=0)
            top, rest = split(both)
            mixer[r] = jnp.concatenate([top, rest], axis=1)

        each(area, prepare)
        links.to_owner(steps, part, near, total, got, sems[:4])
        scale = 1.0 / math.sqrt(NY * NZ) / math.sqrt(KY * KZ)

        def mix(r):
            u = got[pl.ds(r, dp, stride=area), :]
            top, rest = split(u)
            out = mm(jnp.concatenate([top, rest], axis=0), mixer[r])
            wide = 2 * chans
            v = out[:dp, :wide] + out[:dp, wide:] + out[dp:, :wide]
            values[pl.ds(r, dp, stride=area), :] = v * scale

        each(area, mix)
        u_ref[...] = got[...]
        links.from_owner(values, back, spec_ref, sems[4:])


def grad_kernel(
    dp, slab, z_ref, yt_ref, u_ref, grad_ref, part, near, total, got, left, *sems
):
    links = Links(dp, slab)
    step = pl.program_id(0)
    per = z_ref.shape[0]
    chans = part.shape[1] // links.count
    area = links.area
    steps = chans // per

    @pl.when(step == 0)
    def _():
        links.greet()

    links.chunk(step, per, lambda c: z_ref[c], yt_ref[links.me_s], part, near, sems)

    @pl.when(step == pl.num_programs(0) - 1)
    def _():
        def prepare(r):
            turned = u_ref[pl.ds(r, dp, stride=area), :].T
            top, rest = split(jnp.concatenate([turned[:chans], turned[chans:]], axis=1))
            left[r] = jnp.concatenate([top, top, rest], axis=1)

        each(area, prepare)
        links.to_owner(steps, part, near, total, got, sems)
        scale = 1.0 / math.sqrt(NY * NZ) / math.sqrt(KY * KZ) / dp

        def multiply(r):
            g = got[pl.ds(r, dp, stride=area), :]
            low = lax.broadcasted_iota(jnp.int32, g.shape, 1) < chans
            turned = halves_swapped(g)
            top, rest = split(jnp.concatenate([g, jnp.where(low, turned, -turned)], axis=0))
            grad = mm(left[r], jnp.concatenate([top, rest, top], axis=0))
            grad_ref[lax.rem(r, links.per_k), lax.div(r, links.per_k)] = grad * scale

        each(area, multiply)


def point_kernel(
    x_ref, cot_ref, spec_ref, bias_ref, skip_ref, zt_ref, back_ref, yback_ref,
    out_ref, z_ref, left, kron_ref,
):
    step = pl.program_id(0)
    chans, rows = left.shape[:2]
    wide = 2 * KZ
    me_s = lax.axis_index("slab")

    @pl.when(step == 0)
    def _():
        tall = chans * SUB
        part = tall // 4
        spread = one_hot((chans, tall), lambda i, r: i == r // SUB)
        for m in range(4):
            pick = one_hot((part, chans), lambda r, o: (r + m * part) // SUB == o)
            rows_of = lax.dot_general(
                pick, skip_ref[...], (((1,), (1,)), ((), ())), preferred_element_type=jnp.float32
            ).astype(jnp.bfloat16)
            same = one_hot((part, tall), lambda r, s: r % SUB == s % SUB)
            kron_ref[m * part : (m + 1) * part, :] = (
                mm(rows_of, spread).astype(jnp.bfloat16) * same
            )
        yback = yback_ref[me_s]

        def invert(o):
            pairs = spec_ref[pl.ds(pl.multiple_of(o * PAIRS, PAIRS), PAIRS), :]
            v = jnp.concatenate([pairs[:, :wide], pairs[:, wide:]], axis=0)
            turned = jnp.concatenate([-v[:, KZ:], v[:, :KZ]], axis=1)
            top, rest = split(jnp.concatenate([v, turned], axis=0))
            yval = mm(yback, jnp.concatenate([top, rest, top], axis=0))
            ytop, yrest = split(yval)
            b = jnp.full((1, wide), bias_ref[o], jnp.float32)
            b0 = b.astype(jnp.bfloat16).astype(jnp.float32)
            b1 = (b - b0).astype(jnp.bfloat16).astype(jnp.float32)
            lane = lax.broadcasted_iota(jnp.int32, b.shape, 1)
            terms = jnp.where(lane == 0, b0, jnp.where(lane == 1, b1, b - b0 - b1))
            terms = jnp.broadcast_to(terms, (rows, wide)).astype(jnp.bfloat16)
            left[o] = jnp.concatenate([ytop, yrest, ytop, terms], axis=1)

        each(chans, invert)

    here = pl.ds(pl.multiple_of(step * ROWS, ROWS), ROWS)
    field = x_ref[...].astype(jnp.float32)
    terms = left[:, here, :].astype(jnp.float32)
    values, sums = [], []
    for m in range(ROWS // SUB):
        own = slice(m * SUB, (m + 1) * SUB)
        x = field[:, own].reshape(chans * SUB, NZ).astype(jnp.bfloat16)
        term = terms[:, own].reshape(chans * SUB, 4 * wide).astype(jnp.bfloat16)
        pre = mm(kron_ref[...], x) + mm(term, back_ref[...])
        sq = pre * pre
        t = jnp.tanh(pre * (gelu_coef + (gelu_coef * cube_coef) * sq))
        h = 0.5 + 0.5 * t
        value = pre * h
        values.append(value.reshape(chans, SUB, NZ))
        grow = 2.0 * gelu_coef + (6.0 * gelu_coef * cube_coef) * sq
        cot = cot_ref[...].astype(jnp.float32)[:, own].reshape(chans * SUB, NZ)
        slope = cot * (h + value * (0.5 - 0.5 * t) * grow)
        top, rest = split(slope)
        zval = mm(top, zt_ref[...])
        zval = zval[:, :wide] + zval[:, wide:] + mm(rest, zt_ref[:, :wide])
        sums.append(zval.reshape(chans, SUB, wide))
    out_ref[...] = jnp.concatenate(values, axis=1).astype(jnp.bfloat16)
    z_ref[...] = jnp.concatenate(split(jnp.concatenate(sums, axis=1)), axis=2)


def whole(shape):
    return pl.BlockSpec(shape, lambda i: (0,) * len(shape))


def link_scratch(dp, slab, chans):
    area = (KY // dp) * (KZ // slab)
    rows = chans * KY * (KZ // slab) // 64
    wide = 2 * chans
    return [
        pltpu.VMEM((slab, rows, 128), jnp.float32),
        pltpu.VMEM((slab - 1, rows, 128), jnp.float32),
        pltpu.VMEM((dp, area, wide), jnp.float32),
        pltpu.VMEM((dp * area, wide), jnp.float32),
    ]


def link_sems(dp, slab, steps):
    return [
        pltpu.SemaphoreType.DMA((slab - 1, steps)),
        pltpu.SemaphoreType.DMA((slab - 1, steps)),
        pltpu.SemaphoreType.DMA((dp,)),
        pltpu.SemaphoreType.DMA((dp,)),
    ]


def forward_part(field, zt, yt, w_spec, dp, slab):
    chans, rows, length = field.shape
    per = 8
    area = (KY // dp) * (KZ // slab)
    wide = 2 * chans

    def kernel(*refs):
        forward_kernel(dp, slab, *refs)

    return pl.pallas_call(
        kernel,
        grid=(chans // per,),
        in_specs=[
            pl.BlockSpec((per, rows, length), lambda i: (i, 0, 0)),
            whole(zt.shape),
            whole(yt.shape),
            whole(w_spec.shape),
        ],
        out_specs=[whole((chans * PAIRS, 4 * KZ)), whole((dp * area, wide))],
        out_shape=[
            jax.ShapeDtypeStruct((chans * PAIRS, 4 * KZ), jnp.float32),
            jax.ShapeDtypeStruct((dp * area, wide), jnp.float32),
        ],
        scratch_shapes=link_scratch(dp, slab, chans)
        + [
            pltpu.VMEM((area, wide, 2 * wide), jnp.bfloat16),
            pltpu.VMEM((dp * area, wide), jnp.float32),
            pltpu.VMEM((slab, dp, area, wide), jnp.float32),
        ]
        + link_sems(dp, slab, chans // per)
        + link_sems(dp, slab, dp),
        compiler_params=pltpu.CompilerParams(
            vmem_limit_bytes=vmem_bytes, collective_id=0, has_side_effects=True
        ),
    )(field, zt, yt, w_spec)


def grad_part(zsum, yt, u, dp, slab):
    chans, rows, width = zsum.shape
    per = 8
    per_j, per_k = KY // dp, KZ // slab

    def kernel(*refs):
        grad_kernel(dp, slab, *refs)

    return pl.pallas_call(
        kernel,
        grid=(chans // per,),
        in_specs=[
            pl.BlockSpec((per, rows, width), lambda i: (i, 0, 0)),
            whole(yt.shape),
            whole(u.shape),
        ],
        out_specs=whole((per_k, per_j, chans, 2 * chans)),
        out_shape=jax.ShapeDtypeStruct((per_k, per_j, chans, 2 * chans), jnp.float32),
        scratch_shapes=link_scratch(dp, slab, chans)
        + [pltpu.VMEM((per_j * per_k, chans, 6 * dp), jnp.bfloat16)]
        + link_sems(dp, slab, chans // per),
        compiler_params=pltpu.CompilerParams(
            vmem_limit_bytes=vmem_bytes, collective_id=1, has_side_effects=True
        ),
    )(zsum, yt, u)


def point_part(field, cot, spec, bias, skip, zt, back, yback):
    chans, rows, length = field.shape
    rowed = pl.BlockSpec((chans, ROWS, length), lambda i: (0, i, 0))
    return pl.pallas_call(
        point_kernel,
        grid=(rows // ROWS,),
        in_specs=[rowed, rowed, whole(spec.shape), pl.BlockSpec(memory_space=pltpu.SMEM)]
        + [whole(a.shape) for a in (skip, zt, back, yback)],
        out_specs=[rowed, pl.BlockSpec((chans, ROWS, 4 * KZ), lambda i: (0, i, 0))],
        out_shape=[
            jax.ShapeDtypeStruct(field.shape, jnp.bfloat16),
            jax.ShapeDtypeStruct((chans, rows, 4 * KZ), jnp.bfloat16),
        ],
        scratch_shapes=[
            pltpu.VMEM((chans, rows, 8 * KZ), jnp.bfloat16),
            pltpu.VMEM((chans * SUB, chans * SUB), jnp.bfloat16),
        ],
        compiler_params=pltpu.CompilerParams(vmem_limit_bytes=vmem_bytes),
    )(field, cot, spec, bias, skip, zt, back, yback)


def body(snapshots, cotangent, w_spec, first_moment, second_moment, w_skip, bias):
    chans, rows, length = snapshots.shape[1:]
    dp = lax.axis_size("dp")
    slab = lax.axis_size("slab")
    group = 64 * slab // KZ
    mode = np.arange(KY)
    ztop, zrest = halves(z_table())
    ones = np.zeros((2 * KZ, length), ml_dtypes.bfloat16)
    ones[:3] = 1
    back = jnp.asarray(np.concatenate([ztop.T, ztop.T, zrest.T, ones], 0))
    order = np.arange(2 * KZ).reshape(2, slab, -1).transpose(1, 0, 2).reshape(-1)
    zt = jnp.asarray(np.concatenate([ztop[:, order], zrest[:, order]], 1))
    ytop, yrest = halves(y_table(mode.reshape(-1, group).T.reshape(-1)))
    yt = np.concatenate([ytop, yrest], 1).reshape(slab, rows, -1)
    yt = jnp.asarray(np.ascontiguousarray(yt.transpose(0, 2, 1)))
    ytop, yrest = halves(y_table(mode.reshape(-1, 2).T.reshape(-1)))
    yback = jnp.asarray(np.concatenate([ytop, ytop, yrest], 1).reshape(slab, rows, -1))

    spec, u = forward_part(snapshots[0], zt, yt, w_spec, dp, slab)
    layer_out, zsum = point_part(
        snapshots[0], cotangent[0], spec, bias, w_skip, zt, back, yback
    )
    grad = grad_part(zsum, yt, u, dp, slab)
    new_first = 0.9 * first_moment + 0.1 * grad
    new_second = 0.95 * second_moment + 0.05 * grad * grad
    bias_first = 1.0 - 0.9**10
    bias_second = 1.0 - 0.95**10
    new_weights = w_spec - 0.01 * (new_first / bias_first) / (
        jnp.sqrt(new_second / bias_second) + 1e-08
    )
    return (layer_out[None], new_weights, new_first, new_second)


def solution(mesh):
    placed = (
        P("dp", None, "slab", None),
        P("dp", None, "slab", None),
        P("slab", "dp", None, None),
        P("slab", "dp", None, None),
        P("slab", "dp", None, None),
        P(),
        P(),
    )
    return jax.shard_map(
        body,
        mesh=mesh,
        in_specs=placed,
        out_specs=(
            P("dp", None, "slab", None),
            P("slab", "dp", None, None),
            P("slab", "dp", None, None),
            P("slab", "dp", None, None),
        ),
        check_vma=False,
    )
```

```python
import math

import jax
import jax.numpy as jnp
import ml_dtypes
import numpy as np
from jax import lax
from jax.experimental import pallas as pl
from jax.experimental.pallas import tpu as pltpu
from jax.sharding import PartitionSpec as P

NY = 512
NZ = 512
KY = 32
KZ = 32
PAIRS = KY // 2
ROWS = 32
SUB = 8

gelu_coef = 0.7978845608028654
cube_coef = 0.044715
vmem_bytes = 56 * 1024 * 1024
MESH = pl.DeviceIdType.MESH


def halves(table):
    top = table.astype(ml_dtypes.bfloat16)
    rest = (table - top.astype(np.float64)).astype(ml_dtypes.bfloat16)
    return top, rest


def z_table():
    angle = 2.0 * math.pi / NZ * (np.outer(np.arange(NZ), np.arange(KZ)) % NZ)
    return np.concatenate([np.cos(angle), -np.sin(angle)], 1)


def y_table(mode):
    freq = np.where(mode < KY // 2, mode, mode - KY)
    angle = 2.0 * math.pi / NY * (np.outer(np.arange(NY), freq) % NY)
    return np.concatenate([np.cos(angle), np.sin(angle)], 1)


def split(x):
    top = x.astype(jnp.bfloat16)
    return top, (x - top.astype(jnp.float32)).astype(jnp.bfloat16)


def mm(a, b):
    return jnp.dot(a, b, preferred_element_type=jnp.float32)


def one_hot(shape, test):
    rows = lax.broadcasted_iota(jnp.int32, shape, 0)
    columns = lax.broadcasted_iota(jnp.int32, shape, 1)
    return jnp.where(test(rows, columns), 1.0, 0.0).astype(jnp.bfloat16)


def each(count, step):
    per = math.gcd(count, 8)

    @pl.loop(0, count // per)
    def _(i):
        for n in range(per):
            step(i * per + n)


def halves_swapped(x):
    half = x.shape[-1] // 2
    return jnp.concatenate([x[:, half:], x[:, :half]], axis=1)


def y_modes(both, ytab, slab):
    wide = 4 * KZ
    both = mm(ytab, both)
    first = both[: 2 * KY]
    w = first[:, :wide] + first[:, wide:] + both[2 * KY :, :wide]
    per_k = KZ // slab
    group = 64 // per_k
    count = KY // group
    lane = lax.broadcasted_iota(jnp.int32, (KY, wide), 1)
    real = lane % (2 * per_k) < per_k
    sine = w[KY:]
    ahead = jnp.concatenate([sine[:, per_k:], sine[:, :per_k]], axis=1)
    behind = jnp.concatenate([sine[:, wide - per_k :], sine[:, : wide - per_k]], axis=1)
    out = w[:KY] + jnp.where(real, ahead, -behind)

    def piece(g, n):
        return out[g * count : (g + 1) * count, n * 2 * per_k : (n + 1) * 2 * per_k]

    return [
        [
            jnp.concatenate([piece(g, c * slab + s) for g in range(group)], axis=1)
            for s in range(slab)
        ]
        for c in range(2)
    ]


class Links:
    def __init__(self, dp, slab):
        self.dp, self.slab = dp, slab
        self.me_d, self.me_s = lax.axis_index("dp"), lax.axis_index("slab")
        self.per_j, self.per_k = KY // dp, KZ // slab
        self.area = self.per_j * self.per_k
        self.group = 64 // self.per_k
        self.count = KY // self.group

    def greet(self):
        barrier = pltpu.get_barrier_semaphore()

        @pl.loop(1, self.dp)
        def _(t):
            there = lax.rem(self.me_d + t, self.dp)
            pl.semaphore_signal(barrier, inc=1, device_id=(there, self.me_s), device_id_type=MESH)

        for t in range(1, self.slab):
            there = lax.rem(self.me_s + t, self.slab)
            pl.semaphore_signal(barrier, inc=1, device_id=(self.me_d, there), device_id_type=MESH)

    def greeted(self):
        pl.semaphore_wait(pltpu.get_barrier_semaphore(), self.dp + self.slab - 2)

    def copy(self, src, dst, send, recv, d, s):
        return pltpu.make_async_remote_copy(
            src_ref=src, dst_ref=dst, send_sem=send, recv_sem=recv,
            device_id=(d, s), device_id_type=MESH,
        )

    def near_copy(self, step, rows, part, near, sems, t):
        there = lax.rem(self.me_s + t, self.slab)
        own = pl.ds(pl.multiple_of(step * rows, rows), rows)
        return self.copy(
            part.at[there, own], near.at[t - 1, own],
            sems[0].at[t - 1, step], sems[1].at[t - 1, step], self.me_d, there,
        )

    def chunk(self, step, per, halves_of, ytab, part, near, sems):
        rows = per * 2 * self.count
        start = pl.multiple_of(step * rows, rows)
        for n in range(per):
            for c, shares in enumerate(y_modes(halves_of(n), ytab, self.slab)):
                for s, value in enumerate(shares):
                    place = start + (2 * n + c) * self.count
                    part[s, pl.ds(place, self.count), :] = value

        @pl.when(step == 0)
        def _():
            self.greeted()

        for t in range(1, self.slab):
            self.near_copy(step, rows, part, near, sems, t).start()

    def to_owner(self, steps, part, near, total, got, sems):
        far_send, far_recv = sems[2:]
        dp, slab, me_d, me_s, area = self.dp, self.slab, self.me_d, self.me_s, self.area
        rows = part.shape[1] // steps
        chans = part.shape[1] // self.count

        @pl.loop(0, steps)
        def _(step):
            for t in range(1, slab):
                self.near_copy(step, rows, part, near, sems, t).wait_recv()

        def far_copy(d):
            return self.copy(
                total.at[d], got.at[pl.ds(me_d * area, area)],
                far_send.at[d], far_recv.at[me_d], d, me_s,
            )

        owners = self.group // self.per_j
        first = lax.div(lax.rem(me_d + 1, dp), owners)

        @pl.loop(0, self.count)
        def _(n):
            q = lax.rem(first + n, self.count)
            own = pl.ds(q, chans, stride=self.count)
            value = part[me_s, own, :]
            for t in range(1, slab):
                value = value + near[t - 1, own, :]
            turned = value.T
            for g in range(self.group):
                block = turned[2 * g * self.per_k : 2 * (g + 1) * self.per_k]
                place = (g % self.per_j) * self.per_k
                d = q * owners + g // self.per_j
                total[d, place : place + self.per_k, :] = jnp.concatenate(
                    [block[: self.per_k], block[self.per_k :]], axis=1
                )
            for g in range(owners):
                d = q * owners + g

                @pl.when(d != me_d)
                def _():
                    far_copy(d).start()

        got[pl.ds(me_d * area, area), :] = total[me_d]

        @pl.loop(0, dp - 1)
        def _(n):
            src = lax.rem(me_d + dp - 1 - n, dp)
            self.copy(
                total.at[src], got.at[pl.ds(src * area, area)],
                far_send.at[src], far_recv.at[src], src, me_s,
            ).wait_recv()

        @pl.loop(0, steps)
        def _(step):
            for t in range(1, slab):
                self.near_copy(step, rows, part, near, sems, t).wait_send()

        @pl.loop(0, dp - 1)
        def _(n):
            far_copy(lax.rem(me_d + 1 + n, dp)).wait_send()

    def from_owner(self, values, back, spec, sems):
        near_send, near_recv, far_send, far_recv = sems
        dp, slab, me_d, me_s, area = self.dp, self.slab, self.me_d, self.me_s, self.area

        def far_copy(d):
            return self.copy(
                values.at[pl.ds(d * area, area)], back.at[me_s, me_d],
                far_send.at[d], far_recv.at[me_d], d, me_s,
            )

        def relay(d, t):
            there = lax.rem(me_s + t, slab)
            return self.copy(
                back.at[me_s, d], back.at[me_s, d],
                near_send.at[t - 1, d], near_recv.at[t - 1, d], me_d, there,
            )

        @pl.loop(0, dp - 1)
        def _(n):
            far_copy(lax.rem(me_d + 1 + n, dp)).start()

        back[me_s, me_d] = values[pl.ds(me_d * area, area), :]
        for t in range(1, slab):
            relay(me_d, t).start()

        @pl.loop(0, dp - 1)
        def _(n):
            src = lax.rem(me_d + dp - 1 - n, dp)
            self.copy(
                values.at[pl.ds(src * area, area)], back.at[me_s, src],
                far_send.at[src], far_recv.at[src], src, me_s,
            ).wait_recv()
            for t in range(1, slab):
                relay(src, t).start()

        owners = 2 // self.per_j
        first = lax.div(me_d, owners)

        @pl.loop(0, PAIRS)
        def _(n):
            m = lax.rem(first + PAIRS - n, PAIRS)
            for q in range(owners):
                d = m * owners + q
                for t in range(1, slab):
                    source = lax.rem(me_s + slab - t, slab)
                    self.copy(
                        back.at[source, d], back.at[source, d],
                        near_send.at[t - 1, d], near_recv.at[t - 1, d], me_d, source,
                    ).wait_recv()
            self.unpack(back, spec, m)

        @pl.loop(0, dp)
        def _(d):
            for t in range(1, slab):
                relay(d, t).wait_send()

        @pl.loop(0, dp - 1)
        def _(n):
            far_copy(lax.rem(me_d + 1 + n, dp)).wait_send()

    def unpack(self, back, spec, m):
        chans = spec.shape[0] // PAIRS
        blocks = []
        for n in range(2):
            if self.per_j == 2:
                d, place = m, n * self.per_k
            else:
                d, place = m * 2 + n, 0
            rows = jnp.concatenate(
                [back[s, d, place : place + self.per_k, :] for s in range(self.slab)], axis=0
            )
            blocks += [rows[:, :chans], rows[:, chans:]]
        spec[pl.ds(m, chans, stride=PAIRS), :] = jnp.concatenate(blocks, axis=0).T


def forward_kernel(
    dp, slab, x_ref, zt_ref, yt_ref, w_ref, spec_ref, u_ref,
    part, near, total, got, mixer, values, back, *sems,
):
    links = Links(dp, slab)
    step = pl.program_id(0)
    per, _, rows, length = x_ref.shape
    chans = part.shape[1] // links.count
    area = links.area
    steps = chans // per // 2

    @pl.when(step == 0)
    def _():
        links.greet()

    sides = [x_ref[:, c].reshape(per * rows, length) for c in range(2)]
    zval = mm(jnp.concatenate(sides, axis=1), zt_ref[: 2 * length])
    zval = (zval[:, : 4 * KZ] + zval[:, 4 * KZ :]).reshape(per, rows, 4 * KZ)

    def halves_of(n):
        return jnp.concatenate(split(zval[n]), axis=1)

    links.chunk(step, per, halves_of, yt_ref[links.me_s], part, near, sems[:4])

    @pl.when(step == pl.num_programs(0) - 1)
    def _():
        def prepare(r):
            w = w_ref[lax.rem(r, links.per_k), lax.div(r, links.per_k)]
            low = lax.broadcasted_iota(jnp.int32, w.shape, 1) < chans
            turned = halves_swapped(w)
            both = jnp.concatenate([w, jnp.where(low, -turned, turned)], axis=0)
            top, rest = split(both)
            mixer[r] = jnp.concatenate([top, rest], axis=1)

        each(area, prepare)
        links.to_owner(steps, part, near, total, got, sems[:4])
        scale = 1.0 / math.sqrt(NY * NZ) / math.sqrt(KY * KZ)

        def mix(r):
            u = got[pl.ds(r, dp, stride=area), :]
            top, rest = split(u)
            out = mm(jnp.concatenate([top, rest], axis=0), mixer[r])
            wide = 2 * chans
            v = out[:dp, :wide] + out[:dp, wide:] + out[dp:, :wide]
            values[pl.ds(r, dp, stride=area), :] = v * scale

        each(area, mix)
        u_ref[...] = got[...]
        links.from_owner(values, back, spec_ref, sems[4:])


def grad_kernel(
    dp, slab, z_ref, yt_ref, u_ref, grad_ref, part, near, total, got, left, *sems
):
    links = Links(dp, slab)
    step = pl.program_id(0)
    per = z_ref.shape[0]
    chans = part.shape[1] // links.count
    area = links.area
    steps = chans // per // 2

    @pl.when(step == 0)
    def _():
        links.greet()

    links.chunk(step, per, lambda n: z_ref[n], yt_ref[links.me_s], part, near, sems)

    @pl.when(step == pl.num_programs(0) - 1)
    def _():
        def prepare(r):
            turned = u_ref[pl.ds(r, dp, stride=area), :].T
            top, rest = split(jnp.concatenate([turned[:chans], turned[chans:]], axis=1))
            left[r] = jnp.concatenate([top, top, rest], axis=1)

        each(area, prepare)
        links.to_owner(steps, part, near, total, got, sems)
        scale = 1.0 / math.sqrt(NY * NZ) / math.sqrt(KY * KZ) / dp

        def multiply(r):
            g = got[pl.ds(r, dp, stride=area), :]
            low = lax.broadcasted_iota(jnp.int32, g.shape, 1) < chans
            turned = halves_swapped(g)
            top, rest = split(jnp.concatenate([g, jnp.where(low, turned, -turned)], axis=0))
            grad = mm(left[r], jnp.concatenate([top, rest, top], axis=0))
            grad_ref[lax.rem(r, links.per_k), lax.div(r, links.per_k)] = grad * scale

        each(area, multiply)


def point_kernel(
    x_ref, cot_ref, spec_ref, bias_ref, skip_ref, zt_ref, back_ref, yback_ref,
    out_ref, z_ref, left, kron_ref, xs, tops, rests,
):
    step = pl.program_id(0)
    groups, tall = left.shape[:2]
    chans = tall // SUB
    half = tall // 2
    rows = groups * SUB
    wide = 2 * KZ
    me_s = lax.axis_index("slab")

    @pl.when(step == 0)
    def _():
        part = tall // 4
        spread = one_hot((chans, tall), lambda i, r: i == r // SUB)
        for m in range(4):

            def channel(r):
                r = r + m * part
                return r % half // SUB * 2 + r // half

            pick = one_hot((part, chans), lambda r, o: channel(r) == o)
            rows_of = lax.dot_general(
                pick, skip_ref[...], (((1,), (1,)), ((), ())), preferred_element_type=jnp.float32
            ).astype(jnp.bfloat16)
            same = one_hot((part, tall), lambda r, s: r % SUB == s % SUB)
            kron_ref[m * part : (m + 1) * part, :] = (
                mm(rows_of, spread).astype(jnp.bfloat16) * same
            )
        yback = yback_ref[me_s]

        def three(o):
            b = jnp.full((rows, 2 * wide), bias_ref[o], jnp.float32)
            b0 = b.astype(jnp.bfloat16).astype(jnp.float32)
            b1 = (b - b0).astype(jnp.bfloat16).astype(jnp.float32)
            lane = lax.broadcasted_iota(jnp.int32, b.shape, 1) - wide
            return jnp.where(lane == 0, b0, jnp.where(lane == 1, b1, b - b0 - b1))

        def invert(n):
            two = [
                spec_ref[pl.ds(pl.multiple_of((2 * n + c) * PAIRS, PAIRS), PAIRS), :]
                for c in range(2)
            ]
            v = jnp.concatenate(
                [
                    jnp.concatenate([two[0][:, :wide], two[1][:, :wide]], axis=1),
                    jnp.concatenate([two[0][:, wide:], two[1][:, wide:]], axis=1),
                ],
                axis=0,
            )
            turned = jnp.concatenate(
                [-v[:, KZ:wide], v[:, :KZ], -v[:, wide + KZ :], v[:, wide : wide + KZ]], axis=1
            )
            top, rest = split(jnp.concatenate([v, turned], axis=0))
            yval = mm(yback, jnp.concatenate([top, rest, top], axis=0))
            high = yval.astype(jnp.bfloat16).astype(jnp.float32)
            low = yval - high
            high_turned, low_turned = halves_swapped(high), halves_swapped(low)
            first = lax.broadcasted_iota(jnp.int32, high.shape, 1) < wide
            even = [
                jnp.where(first, high, low_turned),
                jnp.where(first, high, three(2 * n)),
            ]
            odd = [
                jnp.where(first, high_turned, low),
                jnp.where(first, high_turned, three(2 * n + 1)),
            ]
            return [
                jnp.concatenate(side, axis=1).reshape(groups, SUB, 4 * wide)
                for side in (even, odd)
            ]

        def invert_two(n):
            one, two = invert(2 * n), invert(2 * n + 1)
            for c in range(2):
                place = pl.multiple_of(c * half + n * 2 * SUB, 2 * SUB)
                left[:, pl.ds(place, 2 * SUB), :] = jnp.concatenate(
                    [one[c], two[c]], axis=1
                ).astype(jnp.bfloat16)

        each(chans // 4, invert_two)

    per = x_ref.shape[1] // SUB
    field = x_ref[...].astype(jnp.float32)
    for m in range(per):
        own = slice(m * SUB, (m + 1) * SUB)
        xs[m] = field[:, own].reshape(tall, NZ).astype(jnp.bfloat16)

    values = [[None] * per for _ in range(2)]

    def piece(c, m):
        these = slice(c * half, (c + 1) * half)
        own = slice(m * SUB, (m + 1) * SUB)
        pre = mm(kron_ref[these, :], xs[m]) + mm(left[step * per + m, these, :], back_ref[...])
        sq = pre * pre
        p = (gelu_coef * cube_coef) * sq
        t = jnp.tanh(pre * (gelu_coef + p))
        h = 0.5 + 0.5 * t
        value = pre * h
        values[c][m] = value.reshape(chans // 2, SUB, NZ)
        grow = 2.0 * gelu_coef + 6.0 * p
        cot = cot_ref[:, c].astype(jnp.float32)[:, own].reshape(half, NZ)
        slope = cot * (h + (value - value * h) * grow)
        top, rest = split(slope)
        tops[m, these, :] = top
        rests[m, these, :] = rest
        if m % 2 == 1:
            both = jnp.concatenate(values[c][m - 1 : m + 1], axis=1).astype(jnp.bfloat16)
            out_ref[:, c, (m - 1) * SUB : (m + 1) * SUB, :] = both

    for m in range(per):
        for c in range(2):
            piece(c, m)

    sides = [
        jnp.concatenate([held[m, c * half : (c + 1) * half, :] for m in range(per)], axis=0)
        for held in (tops, rests)
        for c in range(2)
    ]
    zval = mm(jnp.concatenate(sides, axis=1), zt_ref[...])
    zval = zval[:, : 2 * wide] + zval[:, 2 * wide :]
    sums = [zval[m * half : (m + 1) * half].reshape(chans // 2, SUB, 2 * wide) for m in range(per)]
    z_ref[...] = jnp.concatenate(split(jnp.concatenate(sums, axis=1)), axis=2)


def whole(shape):
    return pl.BlockSpec(shape, lambda i: (0,) * len(shape))


def link_scratch(dp, slab, chans):
    area = (KY // dp) * (KZ // slab)
    rows = chans * KY * (KZ // slab) // 64
    wide = 2 * chans
    return [
        pltpu.VMEM((slab, rows, 128), jnp.float32),
        pltpu.VMEM((slab - 1, rows, 128), jnp.float32),
        pltpu.VMEM((dp, area, wide), jnp.float32),
        pltpu.VMEM((dp * area, wide), jnp.float32),
    ]


def link_sems(dp, slab, steps):
    return [
        pltpu.SemaphoreType.DMA((slab - 1, steps)),
        pltpu.SemaphoreType.DMA((slab - 1, steps)),
        pltpu.SemaphoreType.DMA((dp,)),
        pltpu.SemaphoreType.DMA((dp,)),
    ]


def forward_part(field, zt, yt, w_spec, dp, slab):
    chans, rows, length = field.shape
    per = 8
    area = (KY // dp) * (KZ // slab)
    field = field.reshape(chans // 2, 2, rows, length)
    wide = 2 * chans

    def kernel(*refs):
        forward_kernel(dp, slab, *refs)

    return pl.pallas_call(
        kernel,
        grid=(chans // 2 // per,),
        in_specs=[
            pl.BlockSpec((per, 2, rows, length), lambda i: (i, 0, 0, 0)),
            whole(zt.shape),
            whole(yt.shape),
            whole(w_spec.shape),
        ],
        out_specs=[whole((chans * PAIRS, 4 * KZ)), whole((dp * area, wide))],
        out_shape=[
            jax.ShapeDtypeStruct((chans * PAIRS, 4 * KZ), jnp.float32),
            jax.ShapeDtypeStruct((dp * area, wide), jnp.float32),
        ],
        scratch_shapes=link_scratch(dp, slab, chans)
        + [
            pltpu.VMEM((area, wide, 2 * wide), jnp.bfloat16),
            pltpu.VMEM((dp * area, wide), jnp.float32),
            pltpu.VMEM((slab, dp, area, wide), jnp.float32),
        ]
        + link_sems(dp, slab, chans // 2 // per)
        + link_sems(dp, slab, dp),
        compiler_params=pltpu.CompilerParams(
            vmem_limit_bytes=vmem_bytes, collective_id=0, has_side_effects=True
        ),
    )(field, zt, yt, w_spec)


def grad_part(zsum, yt, u, dp, slab):
    pairs, rows, width = zsum.shape
    chans = 2 * pairs
    per = 8
    per_j, per_k = KY // dp, KZ // slab

    def kernel(*refs):
        grad_kernel(dp, slab, *refs)

    return pl.pallas_call(
        kernel,
        grid=(pairs // per,),
        in_specs=[
            pl.BlockSpec((per, rows, width), lambda i: (i, 0, 0)),
            whole(yt.shape),
            whole(u.shape),
        ],
        out_specs=whole((per_k, per_j, chans, 2 * chans)),
        out_shape=jax.ShapeDtypeStruct((per_k, per_j, chans, 2 * chans), jnp.float32),
        scratch_shapes=link_scratch(dp, slab, chans)
        + [pltpu.VMEM((per_j * per_k, chans, 6 * dp), jnp.bfloat16)]
        + link_sems(dp, slab, chans // 2 // per),
        compiler_params=pltpu.CompilerParams(
            vmem_limit_bytes=vmem_bytes, collective_id=1, has_side_effects=True
        ),
    )(zsum, yt, u)


def point_part(field, cot, spec, bias, skip, zt, back, yback):
    chans, rows, length = field.shape
    paired = (chans // 2, 2, rows, length)
    two = pl.BlockSpec((chans // 2, 2, ROWS, length), lambda i: (0, 0, i, 0))
    held = pltpu.VMEM((ROWS // SUB, chans * SUB, length), jnp.bfloat16)
    out, zsum = pl.pallas_call(
        point_kernel,
        grid=(rows // ROWS,),
        in_specs=[
            pl.BlockSpec((chans, ROWS, length), lambda i: (0, i, 0)),
            two,
            whole(spec.shape),
            pl.BlockSpec(memory_space=pltpu.SMEM),
        ]
        + [whole(a.shape) for a in (skip, zt, back, yback)],
        out_specs=[two, pl.BlockSpec((chans // 2, ROWS, 8 * KZ), lambda i: (0, i, 0))],
        out_shape=[
            jax.ShapeDtypeStruct(paired, jnp.bfloat16),
            jax.ShapeDtypeStruct((chans // 2, rows, 8 * KZ), jnp.bfloat16),
        ],
        scratch_shapes=[
            pltpu.VMEM((rows // SUB, chans * SUB, 8 * KZ), jnp.bfloat16),
            pltpu.VMEM((chans * SUB, chans * SUB), jnp.bfloat16),
            held,
            held,
            held,
        ],
        compiler_params=pltpu.CompilerParams(vmem_limit_bytes=vmem_bytes),
    )(field, cot.reshape(paired), spec, bias, skip, zt, back, yback)
    return out.reshape(field.shape), zsum


def body(snapshots, cotangent, w_spec, first_moment, second_moment, w_skip, bias):
    chans, rows, length = snapshots.shape[1:]
    dp = lax.axis_size("dp")
    slab = lax.axis_size("slab")
    group = 64 * slab // KZ
    mode = np.arange(KY)
    ztop, zrest = halves(z_table())
    ones = np.zeros((2 * KZ, length), ml_dtypes.bfloat16)
    ones[:3] = 1
    back = jnp.asarray(np.concatenate([ztop.T, ztop.T, zrest.T, ones], 0))
    order = np.arange(2 * KZ).reshape(2, slab, -1).transpose(1, 0, 2).reshape(-1)
    ztop, zrest = ztop[:, order], zrest[:, order]
    none = np.zeros_like(ztop)
    zt = [
        [ztop, none, zrest, none],
        [none, ztop, none, zrest],
        [ztop, none, none, none],
        [none, ztop, none, none],
    ]
    zt = jnp.asarray(np.block(zt))
    ytop, yrest = halves(y_table(mode.reshape(-1, group).T.reshape(-1)))
    yt = np.concatenate([ytop, yrest], 1).reshape(slab, rows, -1)
    yt = jnp.asarray(np.ascontiguousarray(yt.transpose(0, 2, 1)))
    ytop, yrest = halves(y_table(mode.reshape(-1, 2).T.reshape(-1)))
    yback = jnp.asarray(np.concatenate([ytop, ytop, yrest], 1).reshape(slab, rows, -1))

    spec, u = forward_part(snapshots[0], zt, yt, w_spec, dp, slab)
    layer_out, zsum = point_part(
        snapshots[0], cotangent[0], spec, bias, w_skip, zt, back, yback
    )
    grad = grad_part(zsum, yt, u, dp, slab)
    new_first = 0.9 * first_moment + 0.1 * grad
    new_second = 0.95 * second_moment + 0.05 * grad * grad
    bias_first = 1.0 - 0.9**10
    bias_second = 1.0 - 0.95**10
    new_weights = w_spec - 0.01 * (new_first / bias_first) / (
        jnp.sqrt(new_second / bias_second) + 1e-08
    )
    return (layer_out[None], new_weights, new_first, new_second)


def solution(mesh):
    placed = (
        P("dp", None, "slab", None),
        P("dp", None, "slab", None),
        P("slab", "dp", None, None),
        P("slab", "dp", None, None),
        P("slab", "dp", None, None),
        P(),
        P(),
    )
    return jax.shard_map(
        body,
        mesh=mesh,
        in_specs=placed,
        out_specs=(
            P("dp", None, "slab", None),
            P("slab", "dp", None, None),
            P("slab", "dp", None, None),
            P("slab", "dp", None, None),
        ),
        check_vma=False,
    )
```

```python
import math

import jax
import jax.numpy as jnp
import ml_dtypes
import numpy as np
from jax import lax
from jax.experimental import pallas as pl
from jax.experimental.pallas import tpu as pltpu
from jax.sharding import PartitionSpec as P

NY = 512
NZ = 512
KY = 32
KZ = 32
PAIRS = KY // 2
ROWS = 32
SUB = 8

gelu_coef = 0.7978845608028654
cube_coef = 0.044715
vmem_bytes = 56 * 1024 * 1024
MESH = pl.DeviceIdType.MESH


def halves(table):
    top = table.astype(ml_dtypes.bfloat16)
    rest = (table - top.astype(np.float64)).astype(ml_dtypes.bfloat16)
    return top, rest


def z_table():
    angle = 2.0 * math.pi / NZ * (np.outer(np.arange(NZ), np.arange(KZ)) % NZ)
    return np.concatenate([np.cos(angle), -np.sin(angle)], 1)


def y_table(mode):
    freq = np.where(mode < KY // 2, mode, mode - KY)
    angle = 2.0 * math.pi / NY * (np.outer(np.arange(NY), freq) % NY)
    return np.concatenate([np.cos(angle), np.sin(angle)], 1)


def split(x):
    top = x.astype(jnp.bfloat16)
    return top, (x - top.astype(jnp.float32)).astype(jnp.bfloat16)


def mm(a, b):
    return jnp.dot(a, b, preferred_element_type=jnp.float32)


def one_hot(shape, test):
    rows = lax.broadcasted_iota(jnp.int32, shape, 0)
    columns = lax.broadcasted_iota(jnp.int32, shape, 1)
    return jnp.where(test(rows, columns), 1.0, 0.0).astype(jnp.bfloat16)


def each(count, step):
    per = math.gcd(count, 8)

    @pl.loop(0, count // per)
    def _(i):
        for n in range(per):
            step(i * per + n)


def halves_swapped(x):
    half = x.shape[-1] // 2
    return jnp.concatenate([x[:, half:], x[:, :half]], axis=1)


def y_modes(both, ytab, slab):
    wide = 4 * KZ
    both = mm(ytab, both)
    first = both[: 2 * KY]
    w = first[:, :wide] + first[:, wide:] + both[2 * KY :, :wide]
    per_k = KZ // slab
    group = 64 // per_k
    count = KY // group
    lane = lax.broadcasted_iota(jnp.int32, (KY, wide), 1)
    real = lane % (2 * per_k) < per_k
    sine = w[KY:]
    ahead = jnp.concatenate([sine[:, per_k:], sine[:, :per_k]], axis=1)
    behind = jnp.concatenate([sine[:, wide - per_k :], sine[:, : wide - per_k]], axis=1)
    out = w[:KY] + jnp.where(real, ahead, -behind)

    def piece(g, n):
        return out[g * count : (g + 1) * count, n * 2 * per_k : (n + 1) * 2 * per_k]

    return [
        [
            jnp.concatenate([piece(g, c * slab + s) for g in range(group)], axis=1)
            for s in range(slab)
        ]
        for c in range(2)
    ]


class Links:
    def __init__(self, dp, slab):
        self.dp, self.slab = dp, slab
        self.me_d, self.me_s = lax.axis_index("dp"), lax.axis_index("slab")
        self.per_j, self.per_k = KY // dp, KZ // slab
        self.area = self.per_j * self.per_k
        self.group = 64 // self.per_k
        self.count = KY // self.group

    def greet(self):
        barrier = pltpu.get_barrier_semaphore()

        @pl.loop(1, self.dp)
        def _(t):
            there = lax.rem(self.me_d + t, self.dp)
            pl.semaphore_signal(barrier, inc=1, device_id=(there, self.me_s), device_id_type=MESH)

        for t in range(1, self.slab):
            there = lax.rem(self.me_s + t, self.slab)
            pl.semaphore_signal(barrier, inc=1, device_id=(self.me_d, there), device_id_type=MESH)

    def greeted(self):
        pl.semaphore_wait(pltpu.get_barrier_semaphore(), self.dp + self.slab - 2)

    def copy(self, src, dst, send, recv, d, s):
        return pltpu.make_async_remote_copy(
            src_ref=src, dst_ref=dst, send_sem=send, recv_sem=recv,
            device_id=(d, s), device_id_type=MESH,
        )

    def near_copy(self, step, rows, part, near, sems, t):
        there = lax.rem(self.me_s + t, self.slab)
        own = pl.ds(pl.multiple_of(step * rows, rows), rows)
        return self.copy(
            part.at[there, own], near.at[t - 1, own],
            sems[0].at[t - 1, step], sems[1].at[t - 1, step], self.me_d, there,
        )

    def chunk(self, step, per, halves_of, ytab, part, near, sems):
        rows = per * 2 * self.count
        start = pl.multiple_of(step * rows, rows)
        for n in range(per):
            for c, shares in enumerate(y_modes(halves_of(n), ytab, self.slab)):
                for s, value in enumerate(shares):
                    place = start + (2 * n + c) * self.count
                    part[s, pl.ds(place, self.count), :] = value

        @pl.when(step == 0)
        def _():
            self.greeted()

        for t in range(1, self.slab):
            self.near_copy(step, rows, part, near, sems, t).start()

    def to_owner(self, steps, part, near, total, got, sems):
        far_send, far_recv = sems[2:]
        dp, slab, me_d, me_s = self.dp, self.slab, self.me_d, self.me_s
        area, some = self.area // 2, self.per_k // 2
        rows = part.shape[1] // steps
        chans = part.shape[1] // self.count // 2
        owners = self.group // self.per_j
        first = lax.div(lax.rem(me_d + 1, dp), owners)

        def place_of(h, d):
            return pl.ds((h * dp + d) * area, area)

        def far_copy(h, d):
            return self.copy(
                total.at[h, d], got.at[place_of(h, me_d)],
                far_send.at[h, d], far_recv.at[h, me_d], d, me_s,
            )

        for h in range(2):

            @pl.loop(h * steps // 2, (h + 1) * steps // 2)
            def _(step):
                for t in range(1, slab):
                    self.near_copy(step, rows, part, near, sems, t).wait_recv()

            @pl.loop(0, self.count)
            def _(n):
                q = lax.rem(first + n, self.count)
                own = pl.ds(h * chans * self.count + q, chans, stride=self.count)
                value = part[me_s, own, :]
                for t in range(1, slab):
                    value = value + near[t - 1, own, :]
                turned = value.T
                for g in range(self.group):
                    block = turned[2 * g * self.per_k : 2 * (g + 1) * self.per_k]
                    place = (g % self.per_j) * some
                    d = q * owners + g // self.per_j
                    total[h, d, place : place + some, :] = jnp.concatenate(
                        [block[n * some : (n + 1) * some] for n in (0, 2, 1, 3)], axis=1
                    )
                for g in range(owners):
                    d = q * owners + g

                    @pl.when(d != me_d)
                    def _():
                        far_copy(h, d).start()

            got[place_of(h, me_d), :] = total[h, me_d]

        for h in range(2):

            @pl.loop(0, dp - 1)
            def _(n):
                src = lax.rem(me_d + dp - 1 - n, dp)
                self.copy(
                    total.at[h, src], got.at[place_of(h, src)],
                    far_send.at[h, src], far_recv.at[h, src], src, me_s,
                ).wait_recv()

        @pl.loop(0, steps)
        def _(step):
            for t in range(1, slab):
                self.near_copy(step, rows, part, near, sems, t).wait_send()

        @pl.loop(0, dp - 1)
        def _(n):
            d = lax.rem(me_d + 1 + n, dp)
            for h in range(2):
                far_copy(h, d).wait_send()

    def owned(self, got, r):
        area, some = self.area // 2, self.per_k // 2
        one = got[pl.ds(r, self.dp, stride=area), :]
        two = got[pl.ds(self.dp * area + r, self.dp, stride=area), :]
        low = lax.broadcasted_iota(jnp.int32, one.shape, 1) < one.shape[1] // 2
        row = lax.div(r, some) * self.per_k + lax.rem(r, some)
        return [
            (row, jnp.where(low, one, halves_swapped(two))),
            (row + some, jnp.where(low, halves_swapped(one), two)),
        ]

    def from_owner(self, values, back, spec, sems):
        near_send, near_recv, far_send, far_recv = sems
        dp, slab, me_d, me_s, area = self.dp, self.slab, self.me_d, self.me_s, self.area

        def far_copy(d):
            return self.copy(
                values.at[pl.ds(d * area, area)], back.at[me_s, me_d],
                far_send.at[d], far_recv.at[me_d], d, me_s,
            )

        def relay(d, t):
            there = lax.rem(me_s + t, slab)
            return self.copy(
                back.at[me_s, d], back.at[me_s, d],
                near_send.at[t - 1, d], near_recv.at[t - 1, d], me_d, there,
            )

        @pl.loop(0, dp - 1)
        def _(n):
            far_copy(lax.rem(me_d + 1 + n, dp)).start()

        back[me_s, me_d] = values[pl.ds(me_d * area, area), :]
        for t in range(1, slab):
            relay(me_d, t).start()

        @pl.loop(0, dp - 1)
        def _(n):
            src = lax.rem(me_d + dp - 1 - n, dp)
            self.copy(
                values.at[pl.ds(src * area, area)], back.at[me_s, src],
                far_send.at[src], far_recv.at[src], src, me_s,
            ).wait_recv()
            for t in range(1, slab):
                relay(src, t).start()

        owners = 2 // self.per_j
        first = lax.div(me_d, owners)

        @pl.loop(0, PAIRS)
        def _(n):
            m = lax.rem(first + PAIRS - n, PAIRS)
            for q in range(owners):
                d = m * owners + q
                for t in range(1, slab):
                    source = lax.rem(me_s + slab - t, slab)
                    self.copy(
                        back.at[source, d], back.at[source, d],
                        near_send.at[t - 1, d], near_recv.at[t - 1, d], me_d, source,
                    ).wait_recv()
            self.unpack(back, spec, m)

        @pl.loop(0, dp)
        def _(d):
            for t in range(1, slab):
                relay(d, t).wait_send()

        @pl.loop(0, dp - 1)
        def _(n):
            far_copy(lax.rem(me_d + 1 + n, dp)).wait_send()

    def unpack(self, back, spec, m):
        chans = spec.shape[0] // PAIRS
        blocks = []
        for n in range(2):
            if self.per_j == 2:
                d, place = m, n * self.per_k
            else:
                d, place = m * 2 + n, 0
            rows = jnp.concatenate(
                [back[s, d, place : place + self.per_k, :] for s in range(self.slab)], axis=0
            )
            blocks += [rows[:, :chans], rows[:, chans:]]
        spec[pl.ds(m, chans, stride=PAIRS), :] = jnp.concatenate(blocks, axis=0).T


def forward_kernel(
    dp, slab, x_ref, zt_ref, yt_ref, w_ref, spec_ref, u_ref,
    part, near, total, got, mixer, values, back, *sems,
):
    links = Links(dp, slab)
    step = pl.program_id(0)
    per, _, rows, length = x_ref.shape
    chans = part.shape[1] // links.count
    area = links.area
    steps = chans // per // 2

    @pl.when(step == 0)
    def _():
        links.greet()

    sides = [x_ref[:, c].reshape(per * rows, length) for c in range(2)]
    zval = mm(jnp.concatenate(sides, axis=1), zt_ref[: 2 * length])
    zval = (zval[:, : 4 * KZ] + zval[:, 4 * KZ :]).reshape(per, rows, 4 * KZ)

    def halves_of(n):
        return jnp.concatenate(split(zval[n]), axis=1)

    links.chunk(step, per, halves_of, yt_ref[links.me_s], part, near, sems[:4])

    @pl.when(step == pl.num_programs(0) - 1)
    def _():
        def prepare(r):
            w = w_ref[lax.rem(r, links.per_k), lax.div(r, links.per_k)]
            low = lax.broadcasted_iota(jnp.int32, w.shape, 1) < chans
            turned = halves_swapped(w)
            turned = jnp.where(low, -turned, turned)
            few = chans // 2
            both = jnp.concatenate([w[:few], turned[:few], w[few:], turned[few:]], axis=0)
            top, rest = split(both)
            mixer[r] = jnp.concatenate([top, rest], axis=1)

        each(area, prepare)
        links.to_owner(steps, part, near, total, got, sems[:4])
        scale = 1.0 / math.sqrt(NY * NZ) / math.sqrt(KY * KZ)

        def mix(pair):
            for r, u in links.owned(got, pair):
                top, rest = split(u)
                out = mm(jnp.concatenate([top, rest], axis=0), mixer[r])
                wide = 2 * chans
                v = out[:dp, :wide] + out[:dp, wide:] + out[dp:, :wide]
                values[pl.ds(r, dp, stride=area), :] = v * scale

        each(area // 2, mix)
        u_ref[...] = got[...]
        links.from_owner(values, back, spec_ref, sems[4:])


def grad_kernel(
    dp, slab, z_ref, yt_ref, u_ref, grad_ref, part, near, total, got, left, *sems
):
    links = Links(dp, slab)
    step = pl.program_id(0)
    per = z_ref.shape[0]
    chans = part.shape[1] // links.count
    area = links.area
    steps = chans // per // 2

    @pl.when(step == 0)
    def _():
        links.greet()

    links.chunk(step, per, lambda n: z_ref[n], yt_ref[links.me_s], part, near, sems)

    @pl.when(step == pl.num_programs(0) - 1)
    def _():
        few = chans // 2

        def prepare(pair):
            for r, u in links.owned(u_ref, pair):
                turned = u.T
                real = jnp.concatenate([turned[:few], turned[2 * few : 3 * few]], axis=0)
                imag = jnp.concatenate([turned[few : 2 * few], turned[3 * few :]], axis=0)
                top, rest = split(jnp.concatenate([real, imag], axis=1))
                left[r] = jnp.concatenate([top, top, rest], axis=1)

        each(area // 2, prepare)
        links.to_owner(steps, part, near, total, got, sems)
        scale = 1.0 / math.sqrt(NY * NZ) / math.sqrt(KY * KZ) / dp

        def multiply(pair):
            for r, g in links.owned(got, pair):
                g = jnp.concatenate(
                    [g[:, n * few : (n + 1) * few] for n in (0, 2, 1, 3)], axis=1
                )
                low = lax.broadcasted_iota(jnp.int32, g.shape, 1) < chans
                turned = halves_swapped(g)
                top, rest = split(jnp.concatenate([g, jnp.where(low, turned, -turned)], axis=0))
                grad = mm(left[r], jnp.concatenate([top, rest, top], axis=0))
                grad_ref[lax.rem(r, links.per_k), lax.div(r, links.per_k)] = grad * scale

        each(area // 2, multiply)


def point_kernel(
    x_ref, cot_ref, spec_ref, bias_ref, skip_ref, zt_ref, back_ref, yback_ref,
    out_ref, z_ref, left, kron_ref, xs, tops, rests,
):
    step = pl.program_id(0)
    groups, tall = left.shape[:2]
    chans = tall // SUB
    half = tall // 2
    rows = groups * SUB
    wide = 2 * KZ
    me_s = lax.axis_index("slab")

    @pl.when(step == 0)
    def _():
        part = tall // 4
        spread = one_hot((chans, tall), lambda i, r: i == r // SUB)
        for m in range(4):

            def channel(r):
                r = r + m * part
                return r % half // SUB * 2 + r // half

            pick = one_hot((part, chans), lambda r, o: channel(r) == o)
            rows_of = lax.dot_general(
                pick, skip_ref[...], (((1,), (1,)), ((), ())), preferred_element_type=jnp.float32
            ).astype(jnp.bfloat16)
            same = one_hot((part, tall), lambda r, s: r % SUB == s % SUB)
            kron_ref[m * part : (m + 1) * part, :] = (
                mm(rows_of, spread).astype(jnp.bfloat16) * same
            )
        yback = yback_ref[me_s]

        def three(o):
            b = jnp.full((rows, 2 * wide), bias_ref[o], jnp.float32)
            b0 = b.astype(jnp.bfloat16).astype(jnp.float32)
            b1 = (b - b0).astype(jnp.bfloat16).astype(jnp.float32)
            lane = lax.broadcasted_iota(jnp.int32, b.shape, 1) - wide
            return jnp.where(lane == 0, b0, jnp.where(lane == 1, b1, b - b0 - b1))

        def invert(n):
            two = [
                spec_ref[pl.ds(pl.multiple_of((2 * n + c) * PAIRS, PAIRS), PAIRS), :]
                for c in range(2)
            ]
            v = jnp.concatenate(
                [
                    jnp.concatenate([two[0][:, :wide], two[1][:, :wide]], axis=1),
                    jnp.concatenate([two[0][:, wide:], two[1][:, wide:]], axis=1),
                ],
                axis=0,
            )
            turned = jnp.concatenate(
                [-v[:, KZ:wide], v[:, :KZ], -v[:, wide + KZ :], v[:, wide : wide + KZ]], axis=1
            )
            top, rest = split(jnp.concatenate([v, turned], axis=0))
            yval = mm(yback, jnp.concatenate([top, rest, top], axis=0))
            high = yval.astype(jnp.bfloat16).astype(jnp.float32)
            low = yval - high
            high_turned, low_turned = halves_swapped(high), halves_swapped(low)
            first = lax.broadcasted_iota(jnp.int32, high.shape, 1) < wide
            even = [
                jnp.where(first, high, low_turned),
                jnp.where(first, high, three(2 * n)),
            ]
            odd = [
                jnp.where(first, high_turned, low),
                jnp.where(first, high_turned, three(2 * n + 1)),
            ]
            return [
                jnp.concatenate(side, axis=1).reshape(groups, SUB, 4 * wide)
                for side in (even, odd)
            ]

        def invert_two(n):
            one, two = invert(2 * n), invert(2 * n + 1)
            for c in range(2):
                place = pl.multiple_of(c * half + n * 2 * SUB, 2 * SUB)
                left[:, pl.ds(place, 2 * SUB), :] = jnp.concatenate(
                    [one[c], two[c]], axis=1
                ).astype(jnp.bfloat16)

        each(chans // 4, invert_two)

    per = x_ref.shape[1] // SUB
    field = x_ref[...].astype(jnp.float32)
    for m in range(per):
        own = slice(m * SUB, (m + 1) * SUB)
        xs[m] = field[:, own].reshape(tall, NZ).astype(jnp.bfloat16)

    values = [[None] * per for _ in range(2)]

    def piece(c, m):
        these = slice(c * half, (c + 1) * half)
        own = slice(m * SUB, (m + 1) * SUB)
        pre = mm(kron_ref[these, :], xs[m]) + mm(left[step * per + m, these, :], back_ref[...])
        sq = pre * pre
        p = (gelu_coef * cube_coef) * sq
        t = jnp.tanh(pre * (gelu_coef + p))
        h = 0.5 + 0.5 * t
        value = pre * h
        values[c][m] = value.reshape(chans // 2, SUB, NZ)
        grow = 2.0 * gelu_coef + 6.0 * p
        cot = cot_ref[:, c].astype(jnp.float32)[:, own].reshape(half, NZ)
        slope = cot * (h + (value - value * h) * grow)
        top, rest = split(slope)
        tops[m, these, :] = top
        rests[m, these, :] = rest
        if m % 2 == 1:
            both = jnp.concatenate(values[c][m - 1 : m + 1], axis=1).astype(jnp.bfloat16)
            out_ref[:, c, (m - 1) * SUB : (m + 1) * SUB, :] = both

    for m in range(per):
        for c in range(2):
            piece(c, m)

    sides = [
        jnp.concatenate([held[m, c * half : (c + 1) * half, :] for m in range(per)], axis=0)
        for held in (tops, rests)
        for c in range(2)
    ]
    zval = mm(jnp.concatenate(sides, axis=1), zt_ref[...])
    zval = zval[:, : 2 * wide] + zval[:, 2 * wide :]
    sums = [zval[m * half : (m + 1) * half].reshape(chans // 2, SUB, 2 * wide) for m in range(per)]
    z_ref[...] = jnp.concatenate(split(jnp.concatenate(sums, axis=1)), axis=2)


def whole(shape):
    return pl.BlockSpec(shape, lambda i: (0,) * len(shape))


def link_scratch(dp, slab, chans):
    area = (KY // dp) * (KZ // slab)
    rows = chans * KY * (KZ // slab) // 64
    wide = 2 * chans
    return [
        pltpu.VMEM((slab, rows, 128), jnp.float32),
        pltpu.VMEM((slab - 1, rows, 128), jnp.float32),
        pltpu.VMEM((2, dp, area // 2, wide), jnp.float32),
        pltpu.VMEM((dp * area, wide), jnp.float32),
    ]


def link_sems(slab, steps, far):
    return [
        pltpu.SemaphoreType.DMA((slab - 1, steps)),
        pltpu.SemaphoreType.DMA((slab - 1, steps)),
        pltpu.SemaphoreType.DMA(far),
        pltpu.SemaphoreType.DMA(far),
    ]


def forward_part(field, zt, yt, w_spec, dp, slab):
    chans, rows, length = field.shape
    per = 8
    area = (KY // dp) * (KZ // slab)
    field = field.reshape(chans // 2, 2, rows, length)
    wide = 2 * chans

    def kernel(*refs):
        forward_kernel(dp, slab, *refs)

    return pl.pallas_call(
        kernel,
        grid=(chans // 2 // per,),
        in_specs=[
            pl.BlockSpec((per, 2, rows, length), lambda i: (i, 0, 0, 0)),
            whole(zt.shape),
            whole(yt.shape),
            whole(w_spec.shape),
        ],
        out_specs=[whole((chans * PAIRS, 4 * KZ)), whole((dp * area, wide))],
        out_shape=[
            jax.ShapeDtypeStruct((chans * PAIRS, 4 * KZ), jnp.float32),
            jax.ShapeDtypeStruct((dp * area, wide), jnp.float32),
        ],
        scratch_shapes=link_scratch(dp, slab, chans)
        + [
            pltpu.VMEM((area, wide, 2 * wide), jnp.bfloat16),
            pltpu.VMEM((dp * area, wide), jnp.float32),
            pltpu.VMEM((slab, dp, area, wide), jnp.float32),
        ]
        + link_sems(slab, chans // 2 // per, (2, dp))
        + link_sems(slab, dp, (dp,)),
        compiler_params=pltpu.CompilerParams(
            vmem_limit_bytes=vmem_bytes, collective_id=0, has_side_effects=True
        ),
    )(field, zt, yt, w_spec)


def grad_part(zsum, yt, u, dp, slab):
    pairs, rows, width = zsum.shape
    chans = 2 * pairs
    per = 8
    per_j, per_k = KY // dp, KZ // slab

    def kernel(*refs):
        grad_kernel(dp, slab, *refs)

    return pl.pallas_call(
        kernel,
        grid=(pairs // per,),
        in_specs=[
            pl.BlockSpec((per, rows, width), lambda i: (i, 0, 0)),
            whole(yt.shape),
            whole(u.shape),
        ],
        out_specs=whole((per_k, per_j, chans, 2 * chans)),
        out_shape=jax.ShapeDtypeStruct((per_k, per_j, chans, 2 * chans), jnp.float32),
        scratch_shapes=link_scratch(dp, slab, chans)
        + [pltpu.VMEM((per_j * per_k, chans, 6 * dp), jnp.bfloat16)]
        + link_sems(slab, chans // 2 // per, (2, dp)),
        compiler_params=pltpu.CompilerParams(
            vmem_limit_bytes=vmem_bytes, collective_id=1, has_side_effects=True
        ),
    )(zsum, yt, u)


def point_part(field, cot, spec, bias, skip, zt, back, yback):
    chans, rows, length = field.shape
    paired = (chans // 2, 2, rows, length)
    two = pl.BlockSpec((chans // 2, 2, ROWS, length), lambda i: (0, 0, i, 0))
    held = pltpu.VMEM((ROWS // SUB, chans * SUB, length), jnp.bfloat16)
    out, zsum = pl.pallas_call(
        point_kernel,
        grid=(rows // ROWS,),
        in_specs=[
            pl.BlockSpec((chans, ROWS, length), lambda i: (0, i, 0)),
            two,
            whole(spec.shape),
            pl.BlockSpec(memory_space=pltpu.SMEM),
        ]
        + [whole(a.shape) for a in (skip, zt, back, yback)],
        out_specs=[two, pl.BlockSpec((chans // 2, ROWS, 8 * KZ), lambda i: (0, i, 0))],
        out_shape=[
            jax.ShapeDtypeStruct(paired, jnp.bfloat16),
            jax.ShapeDtypeStruct((chans // 2, rows, 8 * KZ), jnp.bfloat16),
        ],
        scratch_shapes=[
            pltpu.VMEM((rows // SUB, chans * SUB, 8 * KZ), jnp.bfloat16),
            pltpu.VMEM((chans * SUB, chans * SUB), jnp.bfloat16),
            held,
            held,
            held,
        ],
        compiler_params=pltpu.CompilerParams(vmem_limit_bytes=vmem_bytes),
    )(field, cot.reshape(paired), spec, bias, skip, zt, back, yback)
    return out.reshape(field.shape), zsum


def body(snapshots, cotangent, w_spec, first_moment, second_moment, w_skip, bias):
    chans, rows, length = snapshots.shape[1:]
    dp = lax.axis_size("dp")
    slab = lax.axis_size("slab")
    group = 64 * slab // KZ
    mode = np.arange(KY)
    ztop, zrest = halves(z_table())
    ones = np.zeros((2 * KZ, length), ml_dtypes.bfloat16)
    ones[:3] = 1
    back = jnp.asarray(np.concatenate([ztop.T, ztop.T, zrest.T, ones], 0))
    order = np.arange(2 * KZ).reshape(2, slab, -1).transpose(1, 0, 2).reshape(-1)
    ztop, zrest = ztop[:, order], zrest[:, order]
    none = np.zeros_like(ztop)
    zt = [
        [ztop, none, zrest, none],
        [none, ztop, none, zrest],
        [ztop, none, none, none],
        [none, ztop, none, none],
    ]
    zt = jnp.asarray(np.block(zt))
    ytop, yrest = halves(y_table(mode.reshape(-1, group).T.reshape(-1)))
    yt = np.concatenate([ytop, yrest], 1).reshape(slab, rows, -1)
    yt = jnp.asarray(np.ascontiguousarray(yt.transpose(0, 2, 1)))
    ytop, yrest = halves(y_table(mode.reshape(-1, 2).T.reshape(-1)))
    yback = jnp.asarray(np.concatenate([ytop, ytop, yrest], 1).reshape(slab, rows, -1))

    spec, u = forward_part(snapshots[0], zt, yt, w_spec, dp, slab)
    layer_out, zsum = point_part(
        snapshots[0], cotangent[0], spec, bias, w_skip, zt, back, yback
    )
    grad = grad_part(zsum, yt, u, dp, slab)
    new_first = 0.9 * first_moment + 0.1 * grad
    new_second = 0.95 * second_moment + 0.05 * grad * grad
    bias_first = 1.0 - 0.9**10
    bias_second = 1.0 - 0.95**10
    new_weights = w_spec - 0.01 * (new_first / bias_first) / (
        jnp.sqrt(new_second / bias_second) + 1e-08
    )
    return (layer_out[None], new_weights, new_first, new_second)


def solution(mesh):
    placed = (
        P("dp", None, "slab", None),
        P("dp", None, "slab", None),
        P("slab", "dp", None, None),
        P("slab", "dp", None, None),
        P("slab", "dp", None, None),
        P(),
        P(),
    )
    return jax.shard_map(
        body,
        mesh=mesh,
        in_specs=placed,
        out_specs=(
            P("dp", None, "slab", None),
            P("slab", "dp", None, None),
            P("slab", "dp", None, None),
            P("slab", "dp", None, None),
        ),
        check_vma=False,
    )
```

```python
import math

import jax
import jax.numpy as jnp
import ml_dtypes
import numpy as np
from jax import lax
from jax.experimental import pallas as pl
from jax.experimental.pallas import tpu as pltpu
from jax.sharding import PartitionSpec as P

NY = 512
NZ = 512
KY = 32
KZ = 32
PAIRS = KY // 2
ROWS = 32
SUB = 8

gelu_coef = 0.7978845608028654
cube_coef = 0.044715
vmem_bytes = 56 * 1024 * 1024
MESH = pl.DeviceIdType.MESH


def halves(table):
    top = table.astype(ml_dtypes.bfloat16)
    rest = (table - top.astype(np.float64)).astype(ml_dtypes.bfloat16)
    return top, rest


def z_table():
    angle = 2.0 * math.pi / NZ * (np.outer(np.arange(NZ), np.arange(KZ)) % NZ)
    return np.concatenate([np.cos(angle), -np.sin(angle)], 1)


def y_table(mode):
    freq = np.where(mode < KY // 2, mode, mode - KY)
    angle = 2.0 * math.pi / NY * (np.outer(np.arange(NY), freq) % NY)
    return np.concatenate([np.cos(angle), np.sin(angle)], 1)


def split(x):
    top = x.astype(jnp.bfloat16)
    return top, (x - top.astype(jnp.float32)).astype(jnp.bfloat16)


def mm(a, b):
    return jnp.dot(a, b, preferred_element_type=jnp.float32)


def one_hot(shape, test):
    rows = lax.broadcasted_iota(jnp.int32, shape, 0)
    columns = lax.broadcasted_iota(jnp.int32, shape, 1)
    return jnp.where(test(rows, columns), 1.0, 0.0).astype(jnp.bfloat16)


def each(count, step):
    per = math.gcd(count, 8)

    @pl.loop(0, count // per)
    def _(i):
        for n in range(per):
            step(i * per + n)


def halves_swapped(x):
    half = x.shape[-1] // 2
    return jnp.concatenate([x[:, half:], x[:, :half]], axis=1)


def y_modes(both, ytab, slab):
    wide = 4 * KZ
    both = mm(ytab, both)
    first = both[: 2 * KY]
    w = first[:, :wide] + first[:, wide:] + both[2 * KY :, :wide]
    per_k = KZ // slab
    group = 64 // per_k
    count = KY // group
    lane = lax.broadcasted_iota(jnp.int32, (KY, wide), 1)
    real = lane % (2 * per_k) < per_k
    sine = w[KY:]
    ahead = jnp.concatenate([sine[:, per_k:], sine[:, :per_k]], axis=1)
    behind = jnp.concatenate([sine[:, wide - per_k :], sine[:, : wide - per_k]], axis=1)
    out = w[:KY] + jnp.where(real, ahead, -behind)

    def piece(g, n):
        return out[g * count : (g + 1) * count, n * 2 * per_k : (n + 1) * 2 * per_k]

    return [
        [
            jnp.concatenate([piece(g, c * slab + s) for g in range(group)], axis=1)
            for s in range(slab)
        ]
        for c in range(2)
    ]


class Links:
    def __init__(self, dp, slab):
        self.dp, self.slab = dp, slab
        self.me_d, self.me_s = lax.axis_index("dp"), lax.axis_index("slab")
        self.per_j, self.per_k = KY // dp, KZ // slab
        self.area = self.per_j * self.per_k
        self.group = 64 // self.per_k
        self.count = KY // self.group

    def greet(self):
        barrier = pltpu.get_barrier_semaphore()

        @pl.loop(1, self.dp)
        def _(t):
            there = lax.rem(self.me_d + t, self.dp)
            pl.semaphore_signal(barrier, inc=1, device_id=(there, self.me_s), device_id_type=MESH)

        for t in range(1, self.slab):
            there = lax.rem(self.me_s + t, self.slab)
            pl.semaphore_signal(barrier, inc=1, device_id=(self.me_d, there), device_id_type=MESH)

    def greeted(self):
        pl.semaphore_wait(pltpu.get_barrier_semaphore(), self.dp + self.slab - 2)

    def copy(self, src, dst, send, recv, d, s):
        return pltpu.make_async_remote_copy(
            src_ref=src, dst_ref=dst, send_sem=send, recv_sem=recv,
            device_id=(d, s), device_id_type=MESH,
        )

    def near_copy(self, step, rows, part, near, sems, t):
        there = lax.rem(self.me_s + t, self.slab)
        own = pl.ds(pl.multiple_of(step * rows, rows), rows)
        return self.copy(
            part.at[there, own], near.at[t - 1, own],
            sems[0].at[t - 1, step], sems[1].at[t - 1, step], self.me_d, there,
        )

    def chunk(self, step, per, halves_of, ytab, part, near, sems):
        rows = per * 2 * self.count
        start = pl.multiple_of(step * rows, rows)
        for n in range(per):
            for c, shares in enumerate(y_modes(halves_of(n), ytab, self.slab)):
                for s, value in enumerate(shares):
                    place = start + (2 * n + c) * self.count
                    part[s, pl.ds(place, self.count), :] = value

        @pl.when(step == 0)
        def _():
            self.greeted()

        for t in range(1, self.slab):
            self.near_copy(step, rows, part, near, sems, t).start()

    def to_owner(self, halves, steps, part, near, total, got, sems):
        far_send, far_recv = sems[2:]
        dp, slab, me_d, me_s = self.dp, self.slab, self.me_d, self.me_s
        area, some = self.area // halves, self.per_k // halves
        rows = part.shape[1] // steps
        chans = part.shape[1] // self.count // halves
        parts = [n + c * halves for n in range(halves) for c in range(2)]
        owners = self.group // self.per_j
        first = lax.div(lax.rem(me_d + 1, dp), owners)

        def place_of(h, d):
            return pl.ds((h * dp + d) * area, area)

        def far_copy(h, d):
            return self.copy(
                total.at[h, d], got.at[place_of(h, me_d)],
                far_send.at[h, d], far_recv.at[h, me_d], d, me_s,
            )

        for h in range(halves):

            @pl.loop(h * steps // halves, (h + 1) * steps // halves)
            def _(step):
                for t in range(1, slab):
                    self.near_copy(step, rows, part, near, sems, t).wait_recv()

            @pl.loop(0, self.count)
            def _(n):
                q = lax.rem(first + n, self.count)
                own = pl.ds(h * chans * self.count + q, chans, stride=self.count)
                value = part[me_s, own, :]
                for t in range(1, slab):
                    value = value + near[t - 1, own, :]
                turned = value.T
                for g in range(self.group):
                    block = turned[2 * g * self.per_k : 2 * (g + 1) * self.per_k]
                    place = (g % self.per_j) * some
                    d = q * owners + g // self.per_j
                    total[h, d, place : place + some, :] = jnp.concatenate(
                        [block[n * some : (n + 1) * some] for n in parts], axis=1
                    )
                for g in range(owners):
                    d = q * owners + g

                    @pl.when(d != me_d)
                    def _():
                        far_copy(h, d).start()

            got[place_of(h, me_d), :] = total[h, me_d]

        for h in range(halves):

            @pl.loop(0, dp - 1)
            def _(n):
                src = lax.rem(me_d + dp - 1 - n, dp)
                self.copy(
                    total.at[h, src], got.at[place_of(h, src)],
                    far_send.at[h, src], far_recv.at[h, src], src, me_s,
                ).wait_recv()

        @pl.loop(0, steps)
        def _(step):
            for t in range(1, slab):
                self.near_copy(step, rows, part, near, sems, t).wait_send()

        @pl.loop(0, dp - 1)
        def _(n):
            d = lax.rem(me_d + 1 + n, dp)
            for h in range(halves):
                far_copy(h, d).wait_send()

    def owned(self, got, r):
        area, some = self.area // 2, self.per_k // 2
        one = got[pl.ds(r, self.dp, stride=area), :]
        two = got[pl.ds(self.dp * area + r, self.dp, stride=area), :]
        low = lax.broadcasted_iota(jnp.int32, one.shape, 1) < one.shape[1] // 2
        row = lax.div(r, some) * self.per_k + lax.rem(r, some)
        return [
            (row, jnp.where(low, one, halves_swapped(two))),
            (row + some, jnp.where(low, halves_swapped(one), two)),
        ]

    def from_owner(self, values, back, spec, sems):
        near_send, near_recv, far_send, far_recv = sems
        dp, slab, me_d, me_s, area = self.dp, self.slab, self.me_d, self.me_s, self.area

        def far_copy(d):
            return self.copy(
                values.at[pl.ds(d * area, area)], back.at[me_s, me_d],
                far_send.at[d], far_recv.at[me_d], d, me_s,
            )

        def relay(d, t):
            there = lax.rem(me_s + t, slab)
            return self.copy(
                back.at[me_s, d], back.at[me_s, d],
                near_send.at[t - 1, d], near_recv.at[t - 1, d], me_d, there,
            )

        @pl.loop(0, dp - 1)
        def _(n):
            far_copy(lax.rem(me_d + 1 + n, dp)).start()

        back[me_s, me_d] = values[pl.ds(me_d * area, area), :]
        for t in range(1, slab):
            relay(me_d, t).start()

        @pl.loop(0, dp - 1)
        def _(n):
            src = lax.rem(me_d + dp - 1 - n, dp)
            self.copy(
                values.at[pl.ds(src * area, area)], back.at[me_s, src],
                far_send.at[src], far_recv.at[src], src, me_s,
            ).wait_recv()
            for t in range(1, slab):
                relay(src, t).start()

        owners = 2 // self.per_j
        first = lax.div(me_d, owners)

        @pl.loop(0, PAIRS)
        def _(n):
            m = lax.rem(first + PAIRS - n, PAIRS)
            for q in range(owners):
                d = m * owners + q
                for t in range(1, slab):
                    source = lax.rem(me_s + slab - t, slab)
                    self.copy(
                        back.at[source, d], back.at[source, d],
                        near_send.at[t - 1, d], near_recv.at[t - 1, d], me_d, source,
                    ).wait_recv()
            self.unpack(back, spec, m)

        @pl.loop(0, dp)
        def _(d):
            for t in range(1, slab):
                relay(d, t).wait_send()

        @pl.loop(0, dp - 1)
        def _(n):
            far_copy(lax.rem(me_d + 1 + n, dp)).wait_send()

    def unpack(self, back, spec, m):
        chans = spec.shape[0] // PAIRS
        blocks = []
        for n in range(2):
            if self.per_j == 2:
                d, place = m, n * self.per_k
            else:
                d, place = m * 2 + n, 0
            rows = jnp.concatenate(
                [back[s, d, place : place + self.per_k, :] for s in range(self.slab)], axis=0
            )
            blocks += [rows[:, :chans], rows[:, chans:]]
        spec[pl.ds(m, chans, stride=PAIRS), :] = jnp.concatenate(blocks, axis=0).T


def forward_kernel(
    dp, slab, x_ref, zt_ref, yt_ref, w_ref, spec_ref, u_ref,
    part, near, total, got, mixer, values, back, *sems,
):
    links = Links(dp, slab)
    step = pl.program_id(0)
    per, _, rows, length = x_ref.shape
    chans = part.shape[1] // links.count
    area = links.area
    steps = chans // per // 2

    @pl.when(step == 0)
    def _():
        links.greet()

    sides = [x_ref[:, c].reshape(per * rows, length) for c in range(2)]
    zval = mm(jnp.concatenate(sides, axis=1), zt_ref[: 2 * length])
    zval = (zval[:, : 4 * KZ] + zval[:, 4 * KZ :]).reshape(per, rows, 4 * KZ)

    def halves_of(n):
        return jnp.concatenate(split(zval[n]), axis=1)

    links.chunk(step, per, halves_of, yt_ref[links.me_s], part, near, sems[:4])

    @pl.when(step == pl.num_programs(0) - 1)
    def _():
        def prepare(r):
            w = w_ref[lax.rem(r, links.per_k), lax.div(r, links.per_k)]
            low = lax.broadcasted_iota(jnp.int32, w.shape, 1) < chans
            turned = halves_swapped(w)
            turned = jnp.where(low, -turned, turned)
            few = chans // 2
            both = jnp.concatenate([w[:few], turned[:few], w[few:], turned[few:]], axis=0)
            top, rest = split(both)
            mixer[r] = jnp.concatenate([top, rest], axis=1)

        each(area, prepare)
        links.to_owner(2, steps, part, near, total, got, sems[:4])
        scale = 1.0 / math.sqrt(NY * NZ) / math.sqrt(KY * KZ)

        def mix(pair):
            for r, u in links.owned(got, pair):
                top, rest = split(u)
                out = mm(jnp.concatenate([top, rest], axis=0), mixer[r])
                wide = 2 * chans
                v = out[:dp, :wide] + out[:dp, wide:] + out[dp:, :wide]
                values[pl.ds(r, dp, stride=area), :] = v * scale

        each(area // 2, mix)
        u_ref[...] = got[...]
        links.from_owner(values, back, spec_ref, sems[4:])


def grad_kernel(
    dp, slab, z_ref, yt_ref, u_ref, grad_ref, part, near, total, got, left, *sems
):
    links = Links(dp, slab)
    step = pl.program_id(0)
    per = z_ref.shape[0]
    chans = part.shape[1] // links.count
    area = links.area
    steps = chans // per // 2

    @pl.when(step == 0)
    def _():
        links.greet()

    links.chunk(step, per, lambda n: z_ref[n], yt_ref[links.me_s], part, near, sems)

    @pl.when(step == pl.num_programs(0) - 1)
    def _():
        few = chans // 2

        def prepare(pair):
            for r, u in links.owned(u_ref, pair):
                turned = u.T
                real = jnp.concatenate([turned[:few], turned[2 * few : 3 * few]], axis=0)
                imag = jnp.concatenate([turned[few : 2 * few], turned[3 * few :]], axis=0)
                top, rest = split(jnp.concatenate([real, imag], axis=1))
                left[r] = jnp.concatenate([top, top, rest], axis=1)

        each(area // 2, prepare)
        links.to_owner(1, steps, part, near, total, got, sems)
        scale = 1.0 / math.sqrt(NY * NZ) / math.sqrt(KY * KZ) / dp

        def multiply(r):
            g = got[pl.ds(r, dp, stride=area), :]
            low = lax.broadcasted_iota(jnp.int32, g.shape, 1) < chans
            turned = halves_swapped(g)
            top, rest = split(jnp.concatenate([g, jnp.where(low, turned, -turned)], axis=0))
            grad = mm(left[r], jnp.concatenate([top, rest, top], axis=0))
            grad_ref[lax.rem(r, links.per_k), lax.div(r, links.per_k)] = grad * scale

        each(area, multiply)


def point_kernel(
    x_ref, cot_ref, spec_ref, bias_ref, skip_ref, zt_ref, back_ref, yback_ref,
    out_ref, z_ref, left, kron_ref, xs, tops, rests,
):
    step = pl.program_id(0)
    groups, tall = left.shape[:2]
    chans = tall // SUB
    half = tall // 2
    rows = groups * SUB
    wide = 2 * KZ
    me_s = lax.axis_index("slab")

    @pl.when(step == 0)
    def _():
        part = tall // 4
        spread = one_hot((chans, tall), lambda i, r: i == r // SUB)
        for m in range(4):

            def channel(r):
                r = r + m * part
                return r % half // SUB * 2 + r // half

            pick = one_hot((part, chans), lambda r, o: channel(r) == o)
            rows_of = lax.dot_general(
                pick, skip_ref[...], (((1,), (1,)), ((), ())), preferred_element_type=jnp.float32
            ).astype(jnp.bfloat16)
            same = one_hot((part, tall), lambda r, s: r % SUB == s % SUB)
            kron_ref[m * part : (m + 1) * part, :] = (
                mm(rows_of, spread).astype(jnp.bfloat16) * same
            )
        yback = yback_ref[me_s]

        def three(o):
            b = jnp.full((rows, 2 * wide), bias_ref[o], jnp.float32)
            b0 = b.astype(jnp.bfloat16).astype(jnp.float32)
            b1 = (b - b0).astype(jnp.bfloat16).astype(jnp.float32)
            lane = lax.broadcasted_iota(jnp.int32, b.shape, 1) - wide
            return jnp.where(lane == 0, b0, jnp.where(lane == 1, b1, b - b0 - b1))

        def invert(n):
            two = [
                spec_ref[pl.ds(pl.multiple_of((2 * n + c) * PAIRS, PAIRS), PAIRS), :]
                for c in range(2)
            ]
            v = jnp.concatenate(
                [
                    jnp.concatenate([two[0][:, :wide], two[1][:, :wide]], axis=1),
                    jnp.concatenate([two[0][:, wide:], two[1][:, wide:]], axis=1),
                ],
                axis=0,
            )
            turned = jnp.concatenate(
                [-v[:, KZ:wide], v[:, :KZ], -v[:, wide + KZ :], v[:, wide : wide + KZ]], axis=1
            )
            top, rest = split(jnp.concatenate([v, turned], axis=0))
            yval = mm(yback, jnp.concatenate([top, rest, top], axis=0))
            high = yval.astype(jnp.bfloat16).astype(jnp.float32)
            low = yval - high
            high_turned, low_turned = halves_swapped(high), halves_swapped(low)
            first = lax.broadcasted_iota(jnp.int32, high.shape, 1) < wide
            even = [
                jnp.where(first, high, low_turned),
                jnp.where(first, high, three(2 * n)),
            ]
            odd = [
                jnp.where(first, high_turned, low),
                jnp.where(first, high_turned, three(2 * n + 1)),
            ]
            return [
                jnp.concatenate(side, axis=1).reshape(groups, SUB, 4 * wide)
                for side in (even, odd)
            ]

        def invert_two(n):
            one, two = invert(2 * n), invert(2 * n + 1)
            for c in range(2):
                place = pl.multiple_of(c * half + n * 2 * SUB, 2 * SUB)
                left[:, pl.ds(place, 2 * SUB), :] = jnp.concatenate(
                    [one[c], two[c]], axis=1
                ).astype(jnp.bfloat16)

        each(chans // 4, invert_two)

    per = x_ref.shape[1] // SUB
    field = x_ref[...].astype(jnp.float32)
    for m in range(per):
        own = slice(m * SUB, (m + 1) * SUB)
        xs[m] = field[:, own].reshape(tall, NZ).astype(jnp.bfloat16)

    values = [[None] * per for _ in range(2)]

    def piece(c, m):
        these = slice(c * half, (c + 1) * half)
        own = slice(m * SUB, (m + 1) * SUB)
        pre = mm(kron_ref[these, :], xs[m]) + mm(left[step * per + m, these, :], back_ref[...])
        sq = pre * pre
        p = (gelu_coef * cube_coef) * sq
        t = jnp.tanh(pre * (gelu_coef + p))
        h = 0.5 + 0.5 * t
        value = pre * h
        values[c][m] = value.reshape(chans // 2, SUB, NZ)
        grow = 2.0 * gelu_coef + 6.0 * p
        cot = cot_ref[:, c].astype(jnp.float32)[:, own].reshape(half, NZ)
        slope = cot * (h + (value - value * h) * grow)
        top, rest = split(slope)
        tops[m, these, :] = top
        rests[m, these, :] = rest
        if m % 2 == 1:
            both = jnp.concatenate(values[c][m - 1 : m + 1], axis=1).astype(jnp.bfloat16)
            out_ref[:, c, (m - 1) * SUB : (m + 1) * SUB, :] = both

    for m in range(per):
        for c in range(2):
            piece(c, m)

    sides = [
        jnp.concatenate([held[m, c * half : (c + 1) * half, :] for m in range(per)], axis=0)
        for held in (tops, rests)
        for c in range(2)
    ]
    zval = mm(jnp.concatenate(sides, axis=1), zt_ref[...])
    zval = zval[:, : 2 * wide] + zval[:, 2 * wide :]
    sums = [zval[m * half : (m + 1) * half].reshape(chans // 2, SUB, 2 * wide) for m in range(per)]
    z_ref[...] = jnp.concatenate(split(jnp.concatenate(sums, axis=1)), axis=2)


def whole(shape):
    return pl.BlockSpec(shape, lambda i: (0,) * len(shape))


def link_scratch(halves, dp, slab, chans):
    area = (KY // dp) * (KZ // slab)
    rows = chans * KY * (KZ // slab) // 64
    wide = 2 * chans
    return [
        pltpu.VMEM((slab, rows, 128), jnp.float32),
        pltpu.VMEM((slab - 1, rows, 128), jnp.float32),
        pltpu.VMEM((halves, dp, area // halves, wide), jnp.float32),
        pltpu.VMEM((dp * area, wide), jnp.float32),
    ]


def link_sems(slab, steps, far):
    return [
        pltpu.SemaphoreType.DMA((slab - 1, steps)),
        pltpu.SemaphoreType.DMA((slab - 1, steps)),
        pltpu.SemaphoreType.DMA(far),
        pltpu.SemaphoreType.DMA(far),
    ]


def forward_part(field, zt, yt, w_spec, dp, slab):
    chans, rows, length = field.shape
    per = 8
    area = (KY // dp) * (KZ // slab)
    field = field.reshape(chans // 2, 2, rows, length)
    wide = 2 * chans

    def kernel(*refs):
        forward_kernel(dp, slab, *refs)

    return pl.pallas_call(
        kernel,
        grid=(chans // 2 // per,),
        in_specs=[
            pl.BlockSpec((per, 2, rows, length), lambda i: (i, 0, 0, 0)),
            whole(zt.shape),
            whole(yt.shape),
            whole(w_spec.shape),
        ],
        out_specs=[whole((chans * PAIRS, 4 * KZ)), whole((dp * area, wide))],
        out_shape=[
            jax.ShapeDtypeStruct((chans * PAIRS, 4 * KZ), jnp.float32),
            jax.ShapeDtypeStruct((dp * area, wide), jnp.float32),
        ],
        scratch_shapes=link_scratch(2, dp, slab, chans)
        + [
            pltpu.VMEM((area, wide, 2 * wide), jnp.bfloat16),
            pltpu.VMEM((dp * area, wide), jnp.float32),
            pltpu.VMEM((slab, dp, area, wide), jnp.float32),
        ]
        + link_sems(slab, chans // 2 // per, (2, dp))
        + link_sems(slab, dp, (dp,)),
        compiler_params=pltpu.CompilerParams(
            vmem_limit_bytes=vmem_bytes, collective_id=0, has_side_effects=True
        ),
    )(field, zt, yt, w_spec)


def grad_part(zsum, yt, u, dp, slab):
    pairs, rows, width = zsum.shape
    chans = 2 * pairs
    per = 8
    per_j, per_k = KY // dp, KZ // slab

    def kernel(*refs):
        grad_kernel(dp, slab, *refs)

    return pl.pallas_call(
        kernel,
        grid=(pairs // per,),
        in_specs=[
            pl.BlockSpec((per, rows, width), lambda i: (i, 0, 0)),
            whole(yt.shape),
            whole(u.shape),
        ],
        out_specs=whole((per_k, per_j, chans, 2 * chans)),
        out_shape=jax.ShapeDtypeStruct((per_k, per_j, chans, 2 * chans), jnp.float32),
        scratch_shapes=link_scratch(1, dp, slab, chans)
        + [pltpu.VMEM((per_j * per_k, chans, 6 * dp), jnp.bfloat16)]
        + link_sems(slab, chans // 2 // per, (1, dp)),
        compiler_params=pltpu.CompilerParams(
            vmem_limit_bytes=vmem_bytes, collective_id=1, has_side_effects=True
        ),
    )(zsum, yt, u)


def point_part(field, cot, spec, bias, skip, zt, back, yback):
    chans, rows, length = field.shape
    paired = (chans // 2, 2, rows, length)
    two = pl.BlockSpec((chans // 2, 2, ROWS, length), lambda i: (0, 0, i, 0))
    held = pltpu.VMEM((ROWS // SUB, chans * SUB, length), jnp.bfloat16)
    out, zsum = pl.pallas_call(
        point_kernel,
        grid=(rows // ROWS,),
        in_specs=[
            pl.BlockSpec((chans, ROWS, length), lambda i: (0, i, 0)),
            two,
            whole(spec.shape),
            pl.BlockSpec(memory_space=pltpu.SMEM),
        ]
        + [whole(a.shape) for a in (skip, zt, back, yback)],
        out_specs=[two, pl.BlockSpec((chans // 2, ROWS, 8 * KZ), lambda i: (0, i, 0))],
        out_shape=[
            jax.ShapeDtypeStruct(paired, jnp.bfloat16),
            jax.ShapeDtypeStruct((chans // 2, rows, 8 * KZ), jnp.bfloat16),
        ],
        scratch_shapes=[
            pltpu.VMEM((rows // SUB, chans * SUB, 8 * KZ), jnp.bfloat16),
            pltpu.VMEM((chans * SUB, chans * SUB), jnp.bfloat16),
            held,
            held,
            held,
        ],
        compiler_params=pltpu.CompilerParams(vmem_limit_bytes=vmem_bytes),
    )(field, cot.reshape(paired), spec, bias, skip, zt, back, yback)
    return out.reshape(field.shape), zsum


def body(snapshots, cotangent, w_spec, first_moment, second_moment, w_skip, bias):
    chans, rows, length = snapshots.shape[1:]
    dp = lax.axis_size("dp")
    slab = lax.axis_size("slab")
    group = 64 * slab // KZ
    mode = np.arange(KY)
    ztop, zrest = halves(z_table())
    ones = np.zeros((2 * KZ, length), ml_dtypes.bfloat16)
    ones[:3] = 1
    back = jnp.asarray(np.concatenate([ztop.T, ztop.T, zrest.T, ones], 0))
    order = np.arange(2 * KZ).reshape(2, slab, -1).transpose(1, 0, 2).reshape(-1)
    ztop, zrest = ztop[:, order], zrest[:, order]
    none = np.zeros_like(ztop)
    zt = [
        [ztop, none, zrest, none],
        [none, ztop, none, zrest],
        [ztop, none, none, none],
        [none, ztop, none, none],
    ]
    zt = jnp.asarray(np.block(zt))
    ytop, yrest = halves(y_table(mode.reshape(-1, group).T.reshape(-1)))
    yt = np.concatenate([ytop, yrest], 1).reshape(slab, rows, -1)
    yt = jnp.asarray(np.ascontiguousarray(yt.transpose(0, 2, 1)))
    ytop, yrest = halves(y_table(mode.reshape(-1, 2).T.reshape(-1)))
    yback = jnp.asarray(np.concatenate([ytop, ytop, yrest], 1).reshape(slab, rows, -1))

    spec, u = forward_part(snapshots[0], zt, yt, w_spec, dp, slab)
    layer_out, zsum = point_part(
        snapshots[0], cotangent[0], spec, bias, w_skip, zt, back, yback
    )
    grad = grad_part(zsum, yt, u, dp, slab)
    new_first = 0.9 * first_moment + 0.1 * grad
    new_second = 0.95 * second_moment + 0.05 * grad * grad
    bias_first = 1.0 - 0.9**10
    bias_second = 1.0 - 0.95**10
    new_weights = w_spec - 0.01 * (new_first / bias_first) / (
        jnp.sqrt(new_second / bias_second) + 1e-08
    )
    return (layer_out[None], new_weights, new_first, new_second)


def solution(mesh):
    placed = (
        P("dp", None, "slab", None),
        P("dp", None, "slab", None),
        P("slab", "dp", None, None),
        P("slab", "dp", None, None),
        P("slab", "dp", None, None),
        P(),
        P(),
    )
    return jax.shard_map(
        body,
        mesh=mesh,
        in_specs=placed,
        out_specs=(
            P("dp", None, "slab", None),
            P("slab", "dp", None, None),
            P("slab", "dp", None, None),
            P("slab", "dp", None, None),
        ),
        check_vma=False,
    )
```

```python
import math

import jax
import jax.numpy as jnp
import ml_dtypes
import numpy as np
from jax import lax
from jax.experimental import pallas as pl
from jax.experimental.pallas import tpu as pltpu
from jax.sharding import PartitionSpec as P

NY = 512
NZ = 512
KY = 32
KZ = 32
PAIRS = KY // 2
ROWS = 32
SUB = 8

gelu_coef = 0.7978845608028654
cube_coef = 0.044715
vmem_bytes = 56 * 1024 * 1024
MESH = pl.DeviceIdType.MESH


def halves(table):
    top = table.astype(ml_dtypes.bfloat16)
    rest = (table - top.astype(np.float64)).astype(ml_dtypes.bfloat16)
    return top, rest


def z_table():
    angle = 2.0 * math.pi / NZ * (np.outer(np.arange(NZ), np.arange(KZ)) % NZ)
    return np.concatenate([np.cos(angle), -np.sin(angle)], 1)


def y_table(mode):
    freq = np.where(mode < KY // 2, mode, mode - KY)
    angle = 2.0 * math.pi / NY * (np.outer(np.arange(NY), freq) % NY)
    return np.concatenate([np.cos(angle), np.sin(angle)], 1)


def split(x):
    top = x.astype(jnp.bfloat16)
    return top, (x - top.astype(jnp.float32)).astype(jnp.bfloat16)


def mm(a, b):
    return jnp.dot(a, b, preferred_element_type=jnp.float32)


def one_hot(shape, test):
    rows = lax.broadcasted_iota(jnp.int32, shape, 0)
    columns = lax.broadcasted_iota(jnp.int32, shape, 1)
    return jnp.where(test(rows, columns), 1.0, 0.0).astype(jnp.bfloat16)


def each(count, step):
    per = math.gcd(count, 16)

    @pl.loop(0, count // per)
    def _(i):
        for n in range(per):
            step(i * per + n)


def halves_swapped(x):
    half = x.shape[-1] // 2
    return jnp.concatenate([x[:, half:], x[:, :half]], axis=1)


def y_modes(both, ytab, slab):
    wide = 4 * KZ
    both = mm(ytab, both)
    first = both[: 2 * KY]
    w = first[:, :wide] + first[:, wide:] + both[2 * KY :, :wide]
    per_k = KZ // slab
    group = 64 // per_k
    count = KY // group
    lane = lax.broadcasted_iota(jnp.int32, (KY, wide), 1)
    real = lane % (2 * per_k) < per_k
    sine = w[KY:]
    ahead = jnp.concatenate([sine[:, per_k:], sine[:, :per_k]], axis=1)
    behind = jnp.concatenate([sine[:, wide - per_k :], sine[:, : wide - per_k]], axis=1)
    out = w[:KY] + jnp.where(real, ahead, -behind)

    def piece(g, n):
        return out[g * count : (g + 1) * count, n * 2 * per_k : (n + 1) * 2 * per_k]

    return [
        [
            jnp.concatenate([piece(g, c * slab + s) for g in range(group)], axis=1)
            for s in range(slab)
        ]
        for c in range(2)
    ]


class Links:
    def __init__(self, dp, slab):
        self.dp, self.slab = dp, slab
        self.me_d, self.me_s = lax.axis_index("dp"), lax.axis_index("slab")
        self.per_j, self.per_k = KY // dp, KZ // slab
        self.area = self.per_j * self.per_k
        self.group = 64 // self.per_k
        self.count = KY // self.group

    def greet(self):
        barrier = pltpu.get_barrier_semaphore()

        @pl.loop(1, self.dp)
        def _(t):
            there = lax.rem(self.me_d + t, self.dp)
            pl.semaphore_signal(barrier, inc=1, device_id=(there, self.me_s), device_id_type=MESH)

        for t in range(1, self.slab):
            there = lax.rem(self.me_s + t, self.slab)
            pl.semaphore_signal(barrier, inc=1, device_id=(self.me_d, there), device_id_type=MESH)

    def greeted(self):
        pl.semaphore_wait(pltpu.get_barrier_semaphore(), self.dp + self.slab - 2)

    def copy(self, src, dst, send, recv, d, s):
        return pltpu.make_async_remote_copy(
            src_ref=src, dst_ref=dst, send_sem=send, recv_sem=recv,
            device_id=(d, s), device_id_type=MESH,
        )

    def near_copy(self, step, rows, part, near, sems, t):
        there = lax.rem(self.me_s + t, self.slab)
        own = pl.ds(pl.multiple_of(step * rows, rows), rows)
        return self.copy(
            part.at[there, own], near.at[t - 1, own],
            sems[0].at[t - 1, step], sems[1].at[t - 1, step], self.me_d, there,
        )

    def chunk(self, step, per, halves_of, ytab, part, near, sems):
        rows = per * 2 * self.count
        start = pl.multiple_of(step * rows, rows)
        for n in range(per):
            for c, shares in enumerate(y_modes(halves_of(n), ytab, self.slab)):
                for s, value in enumerate(shares):
                    place = start + (2 * n + c) * self.count
                    part[s, pl.ds(place, self.count), :] = value

        @pl.when(step == 0)
        def _():
            self.greeted()

        for t in range(1, self.slab):
            self.near_copy(step, rows, part, near, sems, t).start()

    def to_owner(self, halves, steps, part, near, total, got, sems, meanwhile):
        far_send, far_recv = sems[2:]
        dp, slab, me_d, me_s = self.dp, self.slab, self.me_d, self.me_s
        area, some = self.area // halves, self.per_k // halves
        rows = part.shape[1] // steps
        chans = part.shape[1] // self.count // halves
        parts = [n + c * halves for n in range(halves) for c in range(2)]
        owners = self.group // self.per_j
        first = lax.div(lax.rem(me_d + 1, dp), owners)

        def place_of(h, d):
            return pl.ds((h * dp + d) * area, area)

        def far_copy(h, d):
            return self.copy(
                total.at[h, d], got.at[place_of(h, me_d)],
                far_send.at[h, d], far_recv.at[h, me_d], d, me_s,
            )

        for h in range(halves):

            @pl.loop(h * steps // halves, (h + 1) * steps // halves)
            def _(step):
                for t in range(1, slab):
                    self.near_copy(step, rows, part, near, sems, t).wait_recv()

            @pl.loop(0, self.count)
            def _(n):
                q = lax.rem(first + n, self.count)
                own = pl.ds(h * chans * self.count + q, chans, stride=self.count)
                value = part[me_s, own, :]
                for t in range(1, slab):
                    value = value + near[t - 1, own, :]
                turned = value.T
                for g in range(self.group):
                    block = turned[2 * g * self.per_k : 2 * (g + 1) * self.per_k]
                    place = (g % self.per_j) * some
                    d = q * owners + g // self.per_j
                    total[h, d, place : place + some, :] = jnp.concatenate(
                        [block[n * some : (n + 1) * some] for n in parts], axis=1
                    )
                for g in range(owners):
                    d = q * owners + g

                    @pl.when(d != me_d)
                    def _():
                        far_copy(h, d).start()

            got[place_of(h, me_d), :] = total[h, me_d]
            if h == halves - 2:
                meanwhile()

        for h in range(halves):

            @pl.loop(0, dp - 1)
            def _(n):
                src = lax.rem(me_d + dp - 1 - n, dp)
                self.copy(
                    total.at[h, src], got.at[place_of(h, src)],
                    far_send.at[h, src], far_recv.at[h, src], src, me_s,
                ).wait_recv()

        @pl.loop(0, steps)
        def _(step):
            for t in range(1, slab):
                self.near_copy(step, rows, part, near, sems, t).wait_send()

        @pl.loop(0, dp - 1)
        def _(n):
            d = lax.rem(me_d + 1 + n, dp)
            for h in range(halves):
                far_copy(h, d).wait_send()

    def owned(self, got, r):
        area, some = self.area // 2, self.per_k // 2
        one = got[pl.ds(r, self.dp, stride=area), :]
        two = got[pl.ds(self.dp * area + r, self.dp, stride=area), :]
        low = lax.broadcasted_iota(jnp.int32, one.shape, 1) < one.shape[1] // 2
        row = lax.div(r, some) * self.per_k + lax.rem(r, some)
        return [
            (row, jnp.where(low, one, halves_swapped(two))),
            (row + some, jnp.where(low, halves_swapped(one), two)),
        ]

    def from_owner(self, values, back, spec, sems):
        near_send, near_recv, far_send, far_recv = sems
        dp, slab, me_d, me_s, area = self.dp, self.slab, self.me_d, self.me_s, self.area

        def far_copy(d):
            return self.copy(
                values.at[pl.ds(d * area, area)], back.at[me_s, me_d],
                far_send.at[d], far_recv.at[me_d], d, me_s,
            )

        def relay(d, t):
            there = lax.rem(me_s + t, slab)
            return self.copy(
                back.at[me_s, d], back.at[me_s, d],
                near_send.at[t - 1, d], near_recv.at[t - 1, d], me_d, there,
            )

        @pl.loop(0, dp - 1)
        def _(n):
            far_copy(lax.rem(me_d + 1 + n, dp)).start()

        back[me_s, me_d] = values[pl.ds(me_d * area, area), :]
        for t in range(1, slab):
            relay(me_d, t).start()

        @pl.loop(0, dp - 1)
        def _(n):
            src = lax.rem(me_d + dp - 1 - n, dp)
            self.copy(
                values.at[pl.ds(src * area, area)], back.at[me_s, src],
                far_send.at[src], far_recv.at[src], src, me_s,
            ).wait_recv()
            for t in range(1, slab):
                relay(src, t).start()

        owners = 2 // self.per_j
        first = lax.div(me_d, owners)

        @pl.loop(0, PAIRS)
        def _(n):
            m = lax.rem(first + PAIRS - n, PAIRS)
            for q in range(owners):
                d = m * owners + q
                for t in range(1, slab):
                    source = lax.rem(me_s + slab - t, slab)
                    self.copy(
                        back.at[source, d], back.at[source, d],
                        near_send.at[t - 1, d], near_recv.at[t - 1, d], me_d, source,
                    ).wait_recv()
            self.unpack(back, spec, m)

        @pl.loop(0, dp)
        def _(d):
            for t in range(1, slab):
                relay(d, t).wait_send()

        @pl.loop(0, dp - 1)
        def _(n):
            far_copy(lax.rem(me_d + 1 + n, dp)).wait_send()

    def unpack(self, back, spec, m):
        chans = spec.shape[0] // PAIRS
        blocks = []
        for n in range(2):
            if self.per_j == 2:
                d, place = m, n * self.per_k
            else:
                d, place = m * 2 + n, 0
            rows = jnp.concatenate(
                [back[s, d, place : place + self.per_k, :] for s in range(self.slab)], axis=0
            )
            blocks += [rows[:, :chans], rows[:, chans:]]
        spec[pl.ds(m, chans, stride=PAIRS), :] = jnp.concatenate(blocks, axis=0).T


def forward_kernel(
    dp, slab, x_ref, zt_ref, yt_ref, w_ref, spec_ref, u_ref,
    part, near, total, got, mixer, values, back, *sems,
):
    links = Links(dp, slab)
    step = pl.program_id(0)
    per, _, rows, length = x_ref.shape
    chans = part.shape[1] // links.count
    area = links.area
    steps = chans // per // 2

    @pl.when(step == 0)
    def _():
        links.greet()

    sides = [x_ref[:, c].reshape(per * rows, length) for c in range(2)]
    zval = mm(jnp.concatenate(sides, axis=1), zt_ref[: 2 * length])
    zval = (zval[:, : 4 * KZ] + zval[:, 4 * KZ :]).reshape(per, rows, 4 * KZ)

    def halves_of(n):
        return jnp.concatenate(split(zval[n]), axis=1)

    links.chunk(step, per, halves_of, yt_ref[links.me_s], part, near, sems[:4])

    @pl.when(step == pl.num_programs(0) - 1)
    def _():
        def prepare(r):
            w = w_ref[lax.rem(r, links.per_k), lax.div(r, links.per_k)]
            low = lax.broadcasted_iota(jnp.int32, w.shape, 1) < chans
            turned = halves_swapped(w)
            turned = jnp.where(low, -turned, turned)
            few = chans // 2
            both = jnp.concatenate([w[:few], turned[:few], w[few:], turned[few:]], axis=0)
            top, rest = split(both)
            mixer[r] = jnp.concatenate([top, rest], axis=1)

        links.to_owner(
            2, steps, part, near, total, got, sems[:4], lambda: each(area, prepare)
        )
        scale = 1.0 / math.sqrt(NY * NZ) / math.sqrt(KY * KZ)

        def mix(pair):
            for r, u in links.owned(got, pair):
                top, rest = split(u)
                out = mm(jnp.concatenate([top, rest], axis=0), mixer[r])
                wide = 2 * chans
                v = out[:dp, :wide] + out[:dp, wide:] + out[dp:, :wide]
                values[pl.ds(r, dp, stride=area), :] = v * scale

        each(area // 2, mix)
        u_ref[...] = got[...]
        links.from_owner(values, back, spec_ref, sems[4:])


def grad_kernel(
    dp, slab, z_ref, yt_ref, u_ref, grad_ref, part, near, total, got, left, *sems
):
    links = Links(dp, slab)
    step = pl.program_id(0)
    per = z_ref.shape[0]
    chans = part.shape[1] // links.count
    area = links.area
    steps = chans // per // 2

    @pl.when(step == 0)
    def _():
        links.greet()

    links.chunk(step, per, lambda n: z_ref[n], yt_ref[links.me_s], part, near, sems)

    @pl.when(step == pl.num_programs(0) - 1)
    def _():
        few = chans // 2

        def prepare(pair):
            for r, u in links.owned(u_ref, pair):
                turned = u.T
                real = jnp.concatenate([turned[:few], turned[2 * few : 3 * few]], axis=0)
                imag = jnp.concatenate([turned[few : 2 * few], turned[3 * few :]], axis=0)
                top, rest = split(jnp.concatenate([real, imag], axis=1))
                left[r] = jnp.concatenate([top, top, rest], axis=1)

        each(area // 2, prepare)
        links.to_owner(1, steps, part, near, total, got, sems, None)
        scale = 1.0 / math.sqrt(NY * NZ) / math.sqrt(KY * KZ) / dp

        def multiply(r):
            g = got[pl.ds(r, dp, stride=area), :]
            low = lax.broadcasted_iota(jnp.int32, g.shape, 1) < chans
            turned = halves_swapped(g)
            top, rest = split(jnp.concatenate([g, jnp.where(low, turned, -turned)], axis=0))
            grad = mm(left[r], jnp.concatenate([top, rest, top], axis=0))
            grad_ref[lax.rem(r, links.per_k), lax.div(r, links.per_k)] = grad * scale

        each(area, multiply)


def point_kernel(
    x_ref, cot_ref, spec_ref, bias_ref, skip_ref, zt_ref, back_ref, yback_ref,
    out_ref, z_ref, left, kron_ref, xs, tops, rests,
):
    step = pl.program_id(0)
    groups, tall = left.shape[:2]
    chans = tall // SUB
    half = tall // 2
    rows = groups * SUB
    wide = 2 * KZ
    me_s = lax.axis_index("slab")

    @pl.when(step == 0)
    def _():
        part = tall // 4
        spread = one_hot((chans, tall), lambda i, r: i == r // SUB)
        for m in range(4):

            def channel(r):
                r = r + m * part
                return r % half // SUB * 2 + r // half

            pick = one_hot((part, chans), lambda r, o: channel(r) == o)
            rows_of = lax.dot_general(
                pick, skip_ref[...], (((1,), (1,)), ((), ())), preferred_element_type=jnp.float32
            ).astype(jnp.bfloat16)
            same = one_hot((part, tall), lambda r, s: r % SUB == s % SUB)
            kron_ref[m * part : (m + 1) * part, :] = (
                mm(rows_of, spread).astype(jnp.bfloat16) * same
            )
        yback = yback_ref[me_s]

        def three(o):
            b = jnp.full((rows, 2 * wide), bias_ref[o], jnp.float32)
            b0 = b.astype(jnp.bfloat16).astype(jnp.float32)
            b1 = (b - b0).astype(jnp.bfloat16).astype(jnp.float32)
            lane = lax.broadcasted_iota(jnp.int32, b.shape, 1) - wide
            return jnp.where(lane == 0, b0, jnp.where(lane == 1, b1, b - b0 - b1))

        def invert(n):
            two = [
                spec_ref[pl.ds(pl.multiple_of((2 * n + c) * PAIRS, PAIRS), PAIRS), :]
                for c in range(2)
            ]
            v = jnp.concatenate(
                [
                    jnp.concatenate([two[0][:, :wide], two[1][:, :wide]], axis=1),
                    jnp.concatenate([two[0][:, wide:], two[1][:, wide:]], axis=1),
                ],
                axis=0,
            )
            turned = jnp.concatenate(
                [-v[:, KZ:wide], v[:, :KZ], -v[:, wide + KZ :], v[:, wide : wide + KZ]], axis=1
            )
            top, rest = split(jnp.concatenate([v, turned], axis=0))
            yval = mm(yback, jnp.concatenate([top, rest, top], axis=0))
            high = yval.astype(jnp.bfloat16).astype(jnp.float32)
            low = yval - high
            high_turned, low_turned = halves_swapped(high), halves_swapped(low)
            first = lax.broadcasted_iota(jnp.int32, high.shape, 1) < wide
            even = [
                jnp.where(first, high, low_turned),
                jnp.where(first, high, three(2 * n)),
            ]
            odd = [
                jnp.where(first, high_turned, low),
                jnp.where(first, high_turned, three(2 * n + 1)),
            ]
            return [
                jnp.concatenate(side, axis=1).reshape(groups, SUB, 4 * wide)
                for side in (even, odd)
            ]

        def invert_two(n):
            one, two = invert(2 * n), invert(2 * n + 1)
            for c in range(2):
                place = pl.multiple_of(c * half + n * 2 * SUB, 2 * SUB)
                left[:, pl.ds(place, 2 * SUB), :] = jnp.concatenate(
                    [one[c], two[c]], axis=1
                ).astype(jnp.bfloat16)

        each(chans // 4, invert_two)

    per = x_ref.shape[1] // SUB
    field = x_ref[...].astype(jnp.float32)
    for m in range(per):
        own = slice(m * SUB, (m + 1) * SUB)
        xs[m] = field[:, own].reshape(tall, NZ).astype(jnp.bfloat16)

    values = [[None] * per for _ in range(2)]

    def piece(c, m):
        these = slice(c * half, (c + 1) * half)
        own = slice(m * SUB, (m + 1) * SUB)
        pre = mm(kron_ref[these, :], xs[m]) + mm(left[step * per + m, these, :], back_ref[...])
        sq = pre * pre
        p = (gelu_coef * cube_coef) * sq
        t = jnp.tanh(pre * (gelu_coef + p))
        h = 0.5 + 0.5 * t
        value = pre * h
        values[c][m] = value.reshape(chans // 2, SUB, NZ)
        grow = 2.0 * gelu_coef + 6.0 * p
        cot = cot_ref[:, c].astype(jnp.float32)[:, own].reshape(half, NZ)
        slope = cot * (h + (value - value * h) * grow)
        top, rest = split(slope)
        tops[m, these, :] = top
        rests[m, these, :] = rest
        if m % 2 == 1:
            both = jnp.concatenate(values[c][m - 1 : m + 1], axis=1).astype(jnp.bfloat16)
            out_ref[:, c, (m - 1) * SUB : (m + 1) * SUB, :] = both

    for m in range(per):
        for c in range(2):
            piece(c, m)

    sides = [
        jnp.concatenate([held[m, c * half : (c + 1) * half, :] for m in range(per)], axis=0)
        for held in (tops, rests)
        for c in range(2)
    ]
    zval = mm(jnp.concatenate(sides, axis=1), zt_ref[...])
    zval = zval[:, : 2 * wide] + zval[:, 2 * wide :]
    sums = [zval[m * half : (m + 1) * half].reshape(chans // 2, SUB, 2 * wide) for m in range(per)]
    z_ref[...] = jnp.concatenate(split(jnp.concatenate(sums, axis=1)), axis=2)


def whole(shape):
    return pl.BlockSpec(shape, lambda i: (0,) * len(shape))


def link_scratch(halves, dp, slab, chans):
    area = (KY // dp) * (KZ // slab)
    rows = chans * KY * (KZ // slab) // 64
    wide = 2 * chans
    return [
        pltpu.VMEM((slab, rows, 128), jnp.float32),
        pltpu.VMEM((slab - 1, rows, 128), jnp.float32),
        pltpu.VMEM((halves, dp, area // halves, wide), jnp.float32),
        pltpu.VMEM((dp * area, wide), jnp.float32),
    ]


def link_sems(slab, steps, far):
    return [
        pltpu.SemaphoreType.DMA((slab - 1, steps)),
        pltpu.SemaphoreType.DMA((slab - 1, steps)),
        pltpu.SemaphoreType.DMA(far),
        pltpu.SemaphoreType.DMA(far),
    ]


def forward_part(field, zt, yt, w_spec, dp, slab):
    chans, rows, length = field.shape
    per = 8
    area = (KY // dp) * (KZ // slab)
    field = field.reshape(chans // 2, 2, rows, length)
    wide = 2 * chans

    def kernel(*refs):
        forward_kernel(dp, slab, *refs)

    return pl.pallas_call(
        kernel,
        grid=(chans // 2 // per,),
        in_specs=[
            pl.BlockSpec((per, 2, rows, length), lambda i: (i, 0, 0, 0)),
            whole(zt.shape),
            whole(yt.shape),
            whole(w_spec.shape),
        ],
        out_specs=[whole((chans * PAIRS, 4 * KZ)), whole((dp * area, wide))],
        out_shape=[
            jax.ShapeDtypeStruct((chans * PAIRS, 4 * KZ), jnp.float32),
            jax.ShapeDtypeStruct((dp * area, wide), jnp.float32),
        ],
        scratch_shapes=link_scratch(2, dp, slab, chans)
        + [
            pltpu.VMEM((area, wide, 2 * wide), jnp.bfloat16),
            pltpu.VMEM((dp * area, wide), jnp.float32),
            pltpu.VMEM((slab, dp, area, wide), jnp.float32),
        ]
        + link_sems(slab, chans // 2 // per, (2, dp))
        + link_sems(slab, dp, (dp,)),
        compiler_params=pltpu.CompilerParams(
            vmem_limit_bytes=vmem_bytes, collective_id=0, has_side_effects=True
        ),
    )(field, zt, yt, w_spec)


def grad_part(zsum, yt, u, dp, slab):
    pairs, rows, width = zsum.shape
    chans = 2 * pairs
    per = 8
    per_j, per_k = KY // dp, KZ // slab

    def kernel(*refs):
        grad_kernel(dp, slab, *refs)

    return pl.pallas_call(
        kernel,
        grid=(pairs // per,),
        in_specs=[
            pl.BlockSpec((per, rows, width), lambda i: (i, 0, 0)),
            whole(yt.shape),
            whole(u.shape),
        ],
        out_specs=whole((per_k, per_j, chans, 2 * chans)),
        out_shape=jax.ShapeDtypeStruct((per_k, per_j, chans, 2 * chans), jnp.float32),
        scratch_shapes=link_scratch(1, dp, slab, chans)
        + [pltpu.VMEM((per_j * per_k, chans, 6 * dp), jnp.bfloat16)]
        + link_sems(slab, chans // 2 // per, (1, dp)),
        compiler_params=pltpu.CompilerParams(
            vmem_limit_bytes=vmem_bytes, collective_id=1, has_side_effects=True
        ),
    )(zsum, yt, u)


def point_part(field, cot, spec, bias, skip, zt, back, yback):
    chans, rows, length = field.shape
    paired = (chans // 2, 2, rows, length)
    two = pl.BlockSpec((chans // 2, 2, ROWS, length), lambda i: (0, 0, i, 0))
    held = pltpu.VMEM((ROWS // SUB, chans * SUB, length), jnp.bfloat16)
    out, zsum = pl.pallas_call(
        point_kernel,
        grid=(rows // ROWS,),
        in_specs=[
            pl.BlockSpec((chans, ROWS, length), lambda i: (0, i, 0)),
            two,
            whole(spec.shape),
            pl.BlockSpec(memory_space=pltpu.SMEM),
        ]
        + [whole(a.shape) for a in (skip, zt, back, yback)],
        out_specs=[two, pl.BlockSpec((chans // 2, ROWS, 8 * KZ), lambda i: (0, i, 0))],
        out_shape=[
            jax.ShapeDtypeStruct(paired, jnp.bfloat16),
            jax.ShapeDtypeStruct((chans // 2, rows, 8 * KZ), jnp.bfloat16),
        ],
        scratch_shapes=[
            pltpu.VMEM((rows // SUB, chans * SUB, 8 * KZ), jnp.bfloat16),
            pltpu.VMEM((chans * SUB, chans * SUB), jnp.bfloat16),
            held,
            held,
            held,
        ],
        compiler_params=pltpu.CompilerParams(vmem_limit_bytes=vmem_bytes),
    )(field, cot.reshape(paired), spec, bias, skip, zt, back, yback)
    return out.reshape(field.shape), zsum


def body(snapshots, cotangent, w_spec, first_moment, second_moment, w_skip, bias):
    chans, rows, length = snapshots.shape[1:]
    dp = lax.axis_size("dp")
    slab = lax.axis_size("slab")
    group = 64 * slab // KZ
    mode = np.arange(KY)
    ztop, zrest = halves(z_table())
    ones = np.zeros((2 * KZ, length), ml_dtypes.bfloat16)
    ones[:3] = 1
    back = jnp.asarray(np.concatenate([ztop.T, ztop.T, zrest.T, ones], 0))
    order = np.arange(2 * KZ).reshape(2, slab, -1).transpose(1, 0, 2).reshape(-1)
    ztop, zrest = ztop[:, order], zrest[:, order]
    none = np.zeros_like(ztop)
    zt = [
        [ztop, none, zrest, none],
        [none, ztop, none, zrest],
        [ztop, none, none, none],
        [none, ztop, none, none],
    ]
    zt = jnp.asarray(np.block(zt))
    ytop, yrest = halves(y_table(mode.reshape(-1, group).T.reshape(-1)))
    yt = np.concatenate([ytop, yrest], 1).reshape(slab, rows, -1)
    yt = jnp.asarray(np.ascontiguousarray(yt.transpose(0, 2, 1)))
    ytop, yrest = halves(y_table(mode.reshape(-1, 2).T.reshape(-1)))
    yback = jnp.asarray(np.concatenate([ytop, ytop, yrest], 1).reshape(slab, rows, -1))

    spec, u = forward_part(snapshots[0], zt, yt, w_spec, dp, slab)
    layer_out, zsum = point_part(
        snapshots[0], cotangent[0], spec, bias, w_skip, zt, back, yback
    )
    grad = grad_part(zsum, yt, u, dp, slab)
    new_first = 0.9 * first_moment + 0.1 * grad
    new_second = 0.95 * second_moment + 0.05 * grad * grad
    bias_first = 1.0 - 0.9**10
    bias_second = 1.0 - 0.95**10
    new_weights = w_spec - 0.01 * (new_first / bias_first) / (
        jnp.sqrt(new_second / bias_second) + 1e-08
    )
    return (layer_out[None], new_weights, new_first, new_second)


def solution(mesh):
    placed = (
        P("dp", None, "slab", None),
        P("dp", None, "slab", None),
        P("slab", "dp", None, None),
        P("slab", "dp", None, None),
        P("slab", "dp", None, None),
        P(),
        P(),
    )
    return jax.shard_map(
        body,
        mesh=mesh,
        in_specs=placed,
        out_specs=(
            P("dp", None, "slab", None),
            P("slab", "dp", None, None),
            P("slab", "dp", None, None),
            P("slab", "dp", None, None),
        ),
        check_vma=False,
    )
```
